256 devices in a mesh: seq: 32 (over z, x_hi, core), batch: 8 (over x_lo, y).
Axes of the slice: x: 4 (x_hi: 2, x_lo: 2; x = x_hi * 2 + x_lo), y: 4, z: 8, core: 2. Of those that a mesh axis runs over, the one named last changes fastest.
Arguments:
- item_ids: int32 [8, 24576], P('batch', 'seq'), may hold values from 0 to 65535
- table: bfloat16 [65536, 512], P('batch'), may hold values from -6 to 6
- tile_user: int32 [8, 192], P('batch'), may hold values from 0 to 47, never falling along the last dimension, each value on 1 to 19 neighbouring positions
- tail_pad: int32 [8, 48], P('batch'), may hold values from 0 to 127
- w_proj: bfloat16 [512, 2048], replicated, may hold values from -0.25 to 0.25
- w_out: bfloat16 [512, 512], replicated, may hold values from -0.25 to 0.25
Outputs:
- mixed: bfloat16 [8, 24576, 512], P('batch', 'seq')
The draws below stay inside these ranges and needn't reach their ends.
Inputs may be any that keep to these rules, and one draw needn't show every extreme that they name: `tile_user`: along each group's tiles the user number never falls; every user of the 48 has 1 to 19 tiles and some user exactly 19, so a user's rows lie within 4 neighbouring shards of seq.
All inputs are finite; a program needn't handle non-finite values.
Results may differ from the reference program's by a relative error of at most 0.0059.
Values may be sent and summed in bfloat16 or wider, within the bound.
No kernel may reach another device: no remote copies, remote signals or barrier semaphores. Data moves between devices by JAX's collectives and lax.ppermute only.
A program may use at most 128 MiB of HBM per device.

```python
import math
import jax
import jax.numpy as jnp
import numpy as np
from jax import lax

D = 512
HEADS = 8
HD = 64
ROWS_DEV = 768
TILE = 128
REACH = 4
GROUPS = 8
SEQ_ROWS = 24576
TILES_GROUP = 192
USERS = 48
MOST_TILES = 19
ITEMS = 65536
N_SEQ = 32


def place_ends(entries, rng, least, largest):
    index_at = [jax.random.randint(jax.random.fold_in(rng, axis), (), 0, length) for axis, length in enumerate(entries.shape)]
    widest = entries.shape.index(max(entries.shape))
    neighbour = index_at[:widest] + [(index_at[widest] + 1) % entries.shape[widest]] + index_at[widest + 1:]
    return entries.at[tuple(index_at)].set(least).at[tuple(neighbour)].set(largest)


def steps_of(stream_key, dims, pieces, least, high):
    factor_of, own = 1.0, jax.random.fold_in(stream_key, 6)
    for axis_at, parts in pieces:
        draws = jnp.exp(jax.random.uniform(jax.random.fold_in(own, axis_at), (parts,), jnp.float32, least / len(pieces), high / len(pieces)))
        factor_of = factor_of * jnp.repeat(draws, dims[axis_at] // parts).reshape([-1 if axis == axis_at else 1 for axis in range(len(dims))])
    return factor_of


def rank_table(amount, lean):
    weights = [(1 << 20) // math.isqrt(standing ** lean) + 1 for standing in range(1, amount + 1)]
    scale = 1 + sum(weights) // (1 << 30)
    return np.cumsum(np.array([max(1, weight // scale) for weight in weights]))


def ranked_ids(rng, extent, number_of, slope):
    table = rank_table(number_of, slope)
    pick = jax.random.randint(jax.random.fold_in(rng, 1), extent, 0, int(table[number_of - 1]))
    rank = jnp.searchsorted(jnp.asarray(table, jnp.int32), pick, side="right")
    return jax.random.permutation(jax.random.fold_in(rng, 2), number_of)[rank].astype(jnp.int32)


def profile(number_of, total, most, lean):
    portions = [(1 << 20) // math.isqrt(standing ** lean) + 1 for standing in range(2, number_of + 1)]
    rest, holding = total - most - (number_of - 1), [1] * (number_of - 1)
    while rest > 0:
        candidates = [i for i in range(number_of - 1) if holding[i] < most]
        whole, left = sum([portions[i] for i in candidates]), rest
        for i in candidates:
            more = min(most - holding[i], max(1, left * portions[i] // whole), rest)
            holding[i] = holding[i] + more
            rest = rest - more
    return np.array([most] + holding)


def uneven_parts(stream_key, number_of, total, reach, skew):
    if number_of == 2:
        one = jax.random.randint(stream_key, (), max(1, total - reach), min(reach, total - 1) + 1)
        return jnp.stack([one, total - one])
    lengths = jnp.asarray(profile(number_of, total, reach, skew), jnp.int32)
    twos = (number_of - 1) // 2
    giver, sink = lengths[1:1 + 2 * twos:2], lengths[2:2 + 2 * twos:2]
    room = jnp.minimum(giver - 1, reach - sink)
    shifted = jax.random.randint(jax.random.fold_in(stream_key, 1), (twos,), 0, 1 << 20) % (room + 1)
    lengths = lengths.at[1:1 + 2 * twos:2].set(giver - shifted).at[2:2 + 2 * twos:2].set(sink + shifted)
    return lengths[jax.random.permutation(jax.random.fold_in(stream_key, 2), number_of)]


def scatter_about(stream_key, extent, width, reach, cuts=(), held_as=jnp.bfloat16):
    values = width * jax.random.normal(stream_key, extent, jnp.float32)
    if cuts:
        values = values * steps_of(stream_key, extent, cuts, -0.22, 0.18)
    return jnp.clip(values, -reach, reach).astype(held_as)


def setup_inputs(seed: int = 0) -> dict:
    key_list = jax.random.split(jax.random.key(seed), 7)
    return {
        "item_ids": place_ends(ranked_ids(key_list[0], (GROUPS, SEQ_ROWS), ITEMS, 2), jax.random.fold_in(key_list[0], 3), 0, ITEMS - 1).astype(jnp.int32),
        "table": scatter_about(key_list[1], (ITEMS, D), 1.0, 6.0, ((0, 8),)),
        "tile_user": jax.vmap(lambda own: jnp.searchsorted(jnp.cumsum(uneven_parts(own, USERS, TILES_GROUP, MOST_TILES, 2)), jnp.arange(TILES_GROUP), side="right"))(jax.random.split(key_list[2], GROUPS)).reshape((GROUPS, TILES_GROUP)).astype(jnp.int32),
        "tail_pad": place_ends(jax.random.randint(key_list[3], (GROUPS, USERS), 0, TILE), jax.random.fold_in(key_list[3], 1), 0, TILE - 1).astype(jnp.int32),
        "w_proj": scatter_about(key_list[4], (D, 4 * D), D ** -0.5, 0.25),
        "w_out": scatter_about(key_list[5], (D, D), D ** -0.5, 0.25),
    }


def layer_norm(values):
    center = values - lax.optimization_barrier(jnp.mean(values, axis=-1, keepdims=True))
    spread = lax.optimization_barrier(jnp.mean(center * center, axis=-1, keepdims=True))
    return center * lax.rsqrt(spread + 1e-05)

def row_layout(tiles, padding):
    count = tiles.shape[0]
    order = jnp.arange(count, dtype=jnp.int32)
    first = lax.optimization_barrier(jnp.sum((tiles[None, :] < tiles[:, None]).astype(jnp.int32), axis=1, dtype=jnp.int32))
    owned = lax.optimization_barrier(jnp.sum((tiles[None, :] == tiles[:, None]).astype(jnp.int32), axis=1, dtype=jnp.int32))
    numbers = jnp.arange(USERS, dtype=jnp.int32)
    tail = lax.optimization_barrier(jnp.sum(jnp.where(tiles[:, None] == numbers[None, :], padding[None, :], 0), axis=1, dtype=jnp.int32))
    limit = owned * TILE - tail
    within = jnp.arange(TILE, dtype=jnp.int32)
    position = ((order - first)[:, None] * TILE + within[None, :]).reshape(-1)
    owner = jnp.repeat(tiles, TILE)
    valid = position < jnp.repeat(limit, TILE)
    return (owner, position, valid)

def reference(item_ids, table, tile_user, tail_pad, w_proj, w_out):
    window = REACH * ROWS_DEV

    def one_group(inputs):
        ids, tiles, padding = inputs
        events = jnp.take(table, ids, axis=0)
        normed = layer_norm(events.astype(jnp.float32)).astype(jnp.bfloat16)
        projected = jax.nn.silu(jnp.dot(normed, w_proj, preferred_element_type=jnp.float32)).astype(jnp.bfloat16)
        projected = lax.optimization_barrier(projected).astype(jnp.float32)
        gate_u = projected[:, :D]
        queries = projected[:, D:2 * D].reshape(SEQ_ROWS, HEADS, HD)
        keys = projected[:, 2 * D:3 * D].reshape(SEQ_ROWS, HEADS, HD)
        values = projected[:, 3 * D:].reshape(SEQ_ROWS, HEADS, HD)
        owner, position, valid = row_layout(tiles, padding)

        def block(index):
            start = (index * ROWS_DEV).astype(jnp.int32)
            begin = jnp.clip(start - (REACH - 1) * ROWS_DEV, 0, SEQ_ROWS - window).astype(jnp.int32)
            query = lax.dynamic_slice_in_dim(queries, start, ROWS_DEV, 0)
            key = lax.dynamic_slice_in_dim(keys, begin, window, 0)
            value = lax.dynamic_slice_in_dim(values, begin, window, 0)
            query_owner = lax.dynamic_slice_in_dim(owner, start, ROWS_DEV, 0)
            query_position = lax.dynamic_slice_in_dim(position, start, ROWS_DEV, 0)
            key_owner = lax.dynamic_slice_in_dim(owner, begin, window, 0)
            key_position = lax.dynamic_slice_in_dim(position, begin, window, 0)
            key_valid = lax.dynamic_slice_in_dim(valid, begin, window, 0)
            allowed = (query_owner[:, None] == key_owner[None, :]) & (key_position[None, :] <= query_position[:, None]) & key_valid[None, :]
            scores = jnp.einsum('qhd,khd->hqk', query, key)
            weights = jnp.where(allowed[None], jax.nn.silu(scores), 0.0).astype(jnp.bfloat16)
            weights = lax.optimization_barrier(weights).astype(jnp.float32)
            return jnp.einsum('hqk,khd->qhd', weights, value)
        attended = lax.map(block, jnp.arange(N_SEQ, dtype=jnp.int32)).reshape(SEQ_ROWS, D)
        gated = (layer_norm(attended) * gate_u).astype(jnp.bfloat16)
        mixed = jnp.dot(gated, w_out, preferred_element_type=jnp.float32) + events.astype(jnp.float32)
        return jnp.where(valid[:, None], mixed, 0.0).astype(jnp.bfloat16)
    return lax.map(one_group, (item_ids, tile_user, tail_pad))
```

```python
import functools

import jax
import jax.numpy as jnp
from jax import lax
from jax.experimental import pallas as pl
from jax.experimental.pallas import tpu as pltpu
from jax.sharding import PartitionSpec as P

HEADS = 8
TILE = 128
REACH = 4
ROOM = 96
SLOTS = 128
MIB = 1 << 20


def vmem():
    return pl.BlockSpec(memory_space=pltpu.VMEM)


def smem():
    return pl.BlockSpec(memory_space=pltpu.SMEM)


def row_norm(values):
    center = values - jnp.mean(values, axis=-1, keepdims=True)
    spread = jnp.mean(center * center, axis=-1, keepdims=True)
    return center * lax.rsqrt(spread + 1e-05)


def half_silu(half):
    return half + half * jnp.tanh(half)


def owner_of(ids, entries, groups):
    owner = jnp.zeros_like(ids)
    for group in range(1, groups):
        owner = owner + jnp.where(ids >= group * entries, 1, 0)
    return owner


def route_kernel(groups, entries, row_ref, list_ref, slot_ref):
    height = row_ref.shape[1]
    ids = row_ref[...]
    lane = lax.broadcasted_iota(jnp.int32, (TILE, height), 1)
    line = lax.broadcasted_iota(jnp.int32, (TILE, height), 0)
    repeat = jnp.zeros((1, height), jnp.int32)
    columns = []
    for start in range(0, height, TILE):
        own_lane = jnp.where(line + start == lane, ids, 0).astype(jnp.float32)
        columns.append(jnp.sum(own_lane, axis=1, keepdims=True).astype(jnp.int32))
        same = (columns[-1] == ids[:, start:]) & (line[:, : height - start] < lane[:, : height - start])
        again = jnp.max(jnp.where(same, 1, 0), axis=0, keepdims=True)
        if start:
            again = jnp.concatenate([jnp.zeros((1, start), jnp.int32), again], axis=1)
        repeat = jnp.maximum(repeat, again)
    fresh = repeat == 0
    owner = owner_of(ids, entries, groups)
    lanes_of = lax.broadcasted_iota(jnp.int32, (groups, height), 0) == owner
    marked = jnp.where(lanes_of & fresh, 1.0, 0.0).astype(jnp.bfloat16)
    rank = jnp.zeros((groups, height), jnp.float32)
    for start in range(0, height, TILE):
        below = jnp.where(line + start < lane, 1.0, 0.0).astype(jnp.bfloat16)
        rank = rank + jnp.dot(
            marked[:, start : start + TILE], below, preferred_element_type=jnp.float32
        )
    place = jnp.sum(jnp.where(lanes_of, rank, 0.0), axis=0, keepdims=True)
    full = jnp.max(jnp.where(fresh, place, 0.0), axis=1, keepdims=True) >= ROOM
    slot = jnp.where(fresh, owner.astype(jnp.float32) * SLOTS + place, 0.0)
    wide = lax.broadcasted_iota(jnp.int32, (TILE, groups * SLOTS), 1)
    wanted = jnp.zeros((1, groups * SLOTS), jnp.int32)
    for start in range(0, height, TILE):
        column = columns[start // TILE]
        mine = jnp.sum(jnp.where(column == ids, slot, 0.0), axis=1, keepdims=True).astype(jnp.int32)
        holder = owner_of(column, entries, groups)
        slot_ref[pl.ds(start, TILE), :] = mine - holder * (SLOTS - ROOM)
        entry = column - holder * entries
        wanted = jnp.maximum(
            wanted, jnp.max(jnp.where(wide == mine, entry, 0), axis=0, keepdims=True)
        )
    place_of = lax.broadcasted_iota(jnp.int32, (1, groups * SLOTS), 1) & (SLOTS - 1)
    list_ref[...] = jnp.where(place_of >= ROOM, jnp.where(full, 1, 0), wanted)


def route(item_ids, groups, entries):
    height = item_ids.shape[1]
    return pl.pallas_call(
        functools.partial(route_kernel, groups, entries),
        out_shape=(
            jax.ShapeDtypeStruct((1, groups * SLOTS), jnp.int32),
            jax.ShapeDtypeStruct((height, 1), jnp.int32),
        ),
        in_specs=[vmem()],
        out_specs=(vmem(), vmem()),
        compiler_params=pltpu.CompilerParams(vmem_limit_bytes=16 * MIB),
        name="route",
    )(item_ids)


def expand_kernel(slot_ref, held_ref, event_ref, normed_ref):
    rows = held_ref.shape[0]
    part = TILE
    wide = lax.broadcasted_iota(jnp.int32, (part, rows), 1)

    def each(half, carry):
        place = pl.ds(pl.multiple_of(half * part, part), part)
        pick = jnp.where(slot_ref[place, :] == wide, 1.0, 0.0).astype(jnp.bfloat16)
        events = jnp.dot(pick, held_ref[...], preferred_element_type=jnp.float32)
        event_ref[place, :] = events.astype(jnp.bfloat16)
        normed_ref[place, :] = row_norm(events).astype(jnp.bfloat16)
        return carry

    lax.fori_loop(0, event_ref.shape[0] // part, each, 0, unroll=True)


def expand(slot, held):
    height, width = slot.shape[0], held.shape[1]
    shape = jax.ShapeDtypeStruct((height, width), jnp.bfloat16)
    return pl.pallas_call(
        expand_kernel,
        out_shape=(shape, shape),
        in_specs=[vmem(), vmem()],
        out_specs=(vmem(), vmem()),
        compiler_params=pltpu.CompilerParams(vmem_limit_bytes=16 * MIB),
        name="expand",
    )(slot, held)


def look_up(item_ids, table, w_proj):
    groups = lax.axis_size("batch")
    height = item_ids.shape[1]
    entries, width = table.shape
    wanted, slot = route(item_ids, groups, entries)
    asked = lax.all_to_all(wanted.reshape(groups, SLOTS), "batch", 0, 0, tiled=True)
    crowded = jnp.max(asked[:, ROOM]) > 0
    picked = jnp.take(table, asked[:, :ROOM].reshape(-1), axis=0, mode="clip")
    held = lax.all_to_all(picked, "batch", 0, 0, tiled=True)
    held, w_half = lax.optimization_barrier((held, w_proj * jnp.bfloat16(0.5)))
    found = expand(slot, held)

    def whole():
        every = lax.all_to_all(
            jnp.broadcast_to(item_ids, (groups, height)), "batch", 0, 0, tiled=True
        )
        local = every.reshape(-1) - lax.axis_index("batch") * entries
        dense = jnp.take(table, local, axis=0, mode="clip")
        dense = lax.all_to_all(dense, "batch", 0, 0, tiled=True).reshape(groups, height, width)
        owner = item_ids[0] // entries
        rows = jnp.zeros((height, width), jnp.bfloat16)
        for group in range(groups):
            rows = jnp.where((owner == group)[:, None], dense[group], rows)
        return rows, row_norm(rows.astype(jnp.float32)).astype(jnp.bfloat16)

    return *lax.cond(crowded, whole, lambda: found), w_half


def earlier_tiles(users_ref, tile, most):
    user = users_ref[0, tile]

    def look(back, count):
        at = tile - back
        here = (at >= 0) & (users_ref[0, jnp.maximum(at, 0)] == user)
        return count + jnp.where(here, 1, 0)

    return lax.fori_loop(1, most + 1, look, jnp.int32(0))


def rows_at(tile):
    return pl.ds(pl.multiple_of(tile * TILE, TILE), TILE)


def stack_heads(block, stack_ref, first_tile):
    lane = lax.broadcasted_iota(jnp.int32, (TILE, TILE), 1)
    heads = (lane < TILE // 2, lane >= TILE // 2)
    masks = [jnp.where(head, 1.0, 0.0).astype(jnp.bfloat16) for head in heads]
    for tile in range(block.shape[0] // TILE):
        for at in range(block.shape[1] // TILE):
            both = block[tile * TILE : (tile + 1) * TILE, at * TILE : (at + 1) * TILE]
            for which in range(2):
                place = pl.ds(pl.multiple_of((first_tile + tile) * 2 * TILE, TILE) + which * TILE, TILE)
                stack_ref[at, place, :] = both * masks[which]


def attend(query_ref, key_ref, value_ref, total_ref, rows, places, mask_ref=None, fresh=False):
    for at in range(key_ref.shape[0]):
        columns = slice(at * TILE, (at + 1) * TILE)
        half = lax.dot_general(
            query_ref[rows, columns],
            key_ref[at, places, :],
            (((1,), (1,)), ((), ())),
            preferred_element_type=jnp.float32,
        )
        weights = half_silu(half).astype(jnp.bfloat16)
        if mask_ref is not None:
            weights = weights * mask_ref[...]
        part = jnp.dot(weights, value_ref[at, places, :], preferred_element_type=jnp.float32)
        if fresh:
            total_ref[rows, columns] = part
        else:
            total_ref[rows, columns] += part


def project(normed, proj_ref, at, width):
    half = jnp.dot(
        normed, proj_ref[:, at * width : (at + 1) * width], preferred_element_type=jnp.float32
    )
    return half_silu(half).astype(jnp.bfloat16)


def own_kernel(
    shard_ref,
    users_ref,
    normed_ref,
    proj_ref,
    gate_ref,
    query_ref,
    total_ref,
    key_ref,
    value_ref,
    mask_ref,
):
    height, width = query_ref.shape
    tiles = height // TILE
    part = height // 2
    base = shard_ref[0, 0] * tiles

    def prepare(half, carry):
        rows = pl.ds(pl.multiple_of(half * part, part), part)
        normed = normed_ref[rows, :]
        gate_ref[rows, :] = project(normed, proj_ref, 0, width)
        query_ref[rows, :] = project(normed, proj_ref, 1, width) * jnp.bfloat16(0.5)
        stack_heads(project(normed, proj_ref, 2, width), key_ref, half * (tiles // 2))
        stack_heads(project(normed, proj_ref, 3, width), value_ref, half * (tiles // 2))
        return carry

    lax.fori_loop(0, 2, prepare, 0)

    line = lax.broadcasted_iota(jnp.int32, (TILE, 2 * part), 0)
    lane = lax.broadcasted_iota(jnp.int32, (TILE, 2 * part), 1)
    key_row = lax.shift_right_logical(lane, 8) * TILE + (lane & (TILE - 1))

    def block(query_half, key_half, fresh):
        def look(tile, carry):
            at = query_half * (tiles // 2) + tile
            first = at - earlier_tiles(users_ref, base + at, tiles - 1)
            least = (first - key_half * (tiles // 2)) * TILE
            most = line + (tile + (query_half - key_half) * (tiles // 2)) * TILE
            seen = (key_row >= least) & (key_row <= most)
            mask_ref[rows_at(tile), :] = jnp.where(seen, 1.0, 0.0).astype(jnp.bfloat16)
            return carry

        lax.fori_loop(0, tiles // 2, look, 0)
        attend(
            query_ref,
            key_ref,
            value_ref,
            total_ref,
            pl.ds(pl.multiple_of(query_half * part, part), part),
            pl.ds(pl.multiple_of(key_half * 2 * part, part), 2 * part),
            mask_ref,
            fresh,
        )

    def same(half, carry):
        block(half, half, True)
        return carry

    lax.fori_loop(0, 2, same, 0)
    middle = base + tiles // 2

    @pl.when(users_ref[0, middle] == users_ref[0, middle - 1])
    def _():
        block(1, 0, False)


def own(shard, users, normed, w_proj):
    height, width = normed.shape
    tiles, pairs = height // TILE, width // TILE
    return pl.pallas_call(
        own_kernel,
        out_shape=(
            jax.ShapeDtypeStruct((height, width), jnp.bfloat16),
            jax.ShapeDtypeStruct((height, width), jnp.bfloat16),
            jax.ShapeDtypeStruct((height, width), jnp.float32),
        ),
        in_specs=[smem(), smem(), vmem(), vmem()],
        out_specs=(vmem(), vmem(), vmem()),
        scratch_shapes=[
            pltpu.VMEM((pairs, tiles * 2 * TILE, TILE), jnp.bfloat16),
            pltpu.VMEM((pairs, tiles * 2 * TILE, TILE), jnp.bfloat16),
            pltpu.VMEM((height // 2, height), jnp.bfloat16),
        ],
        compiler_params=pltpu.CompilerParams(vmem_limit_bytes=24 * MIB),
        cost_estimate=pl.CostEstimate(flops=10**6, bytes_accessed=10**5, transcendentals=0),
        name="own",
    )(shard, users, normed, w_proj)


def add_half(
    normed, half, begin, asking, proj_ref, query_ref, total_ref, key_ref, value_ref
):
    part, width = normed.shape
    line = lax.broadcasted_iota(jnp.int32, (part, width), 0) + half * part
    values = project(normed, proj_ref, 1, width)
    values = jnp.where(line >= begin, values.astype(jnp.float32), 0.0)
    stack_heads(project(normed, proj_ref, 0, width), key_ref, 0)
    stack_heads(values.astype(jnp.bfloat16), value_ref, 0)

    def query(at, carry):
        attend(
            query_ref,
            key_ref,
            value_ref,
            total_ref,
            pl.ds(pl.multiple_of(at * part, part), part),
            pl.ds(0, 2 * part),
        )
        return carry

    lax.fori_loop(0, jnp.where(asking * TILE > part, 2, 1), query, 0)


def add_earlier(
    block_ref, distance, needed, asking, proj_ref, query_ref, total_ref, key_ref, value_ref
):
    height = query_ref.shape[0]
    part = height // 2
    used = used_of(needed, distance, height // TILE)

    @pl.when(used > 0)
    def _():
        total_ref[...] = jnp.zeros_like(total_ref)

    def each(half, carry):
        add_half(
            block_ref[pl.ds(pl.multiple_of(half * part, part), part), :],
            half,
            height - used * TILE,
            asking,
            proj_ref,
            query_ref,
            total_ref,
            key_ref,
            value_ref,
        )
        return carry

    lax.fori_loop(jnp.where(used * TILE > part, 0, 1), jnp.where(used > 0, 2, 0), each, 0)


def used_of(needed, distance, tiles):
    return jnp.clip(needed - tiles * (distance - 1), 0, tiles)


def reach(shard_ref, users_ref, tiles):
    base = shard_ref[0, 0] * tiles
    needed = earlier_tiles(users_ref, base, (REACH - 1) * tiles)
    asking = jnp.int32(0)
    for tile in range(tiles):
        asking = asking + jnp.where(users_ref[0, base + tile] == users_ref[0, base], 1, 0)
    return base, needed, asking


def early_kernel(
    shard_ref,
    users_ref,
    block_ref,
    proj_ref,
    query_ref,
    total_ref,
    key_ref,
    value_ref,
):
    _, needed, asking = reach(shard_ref, users_ref, query_ref.shape[0] // TILE)
    add_earlier(
        block_ref, 2, needed, asking, proj_ref, query_ref, total_ref, key_ref, value_ref
    )


def middle_kernel(
    shard_ref,
    users_ref,
    block_ref,
    proj_ref,
    query_ref,
    total_ref,
    key_ref,
    value_ref,
):
    _, needed, asking = reach(shard_ref, users_ref, query_ref.shape[0] // TILE)
    add_earlier(
        block_ref,
        3 - 2 * lax.rem(shard_ref[0, 0], 2),
        needed,
        asking,
        proj_ref,
        query_ref,
        total_ref,
        key_ref,
        value_ref,
    )


def late_kernel(
    shard_ref,
    users_ref,
    pad_ref,
    block_ref,
    proj_ref,
    query_ref,
    gate_ref,
    own_ref,
    early_ref,
    middle_ref,
    event_ref,
    out_proj_ref,
    out_ref,
    total_ref,
    key_ref,
    value_ref,
):
    height, width = query_ref.shape
    tiles = height // TILE
    count = users_ref.shape[1]
    base, needed, asking = reach(shard_ref, users_ref, tiles)
    core = lax.rem(shard_ref[0, 0], 2)
    add_earlier(
        block_ref,
        1 + 2 * core,
        needed,
        asking,
        proj_ref,
        query_ref,
        total_ref,
        key_ref,
        value_ref,
    )
    parts = (
        (early_ref, used_of(needed, 2, tiles)),
        (middle_ref, used_of(needed, 3 - 2 * core, tiles)),
        (total_ref, used_of(needed, 1 + 2 * core, tiles)),
    )
    part = height // 2

    line = lax.broadcasted_iota(jnp.int32, (TILE, width), 0)

    def finish(half, carry):
        rows = pl.ds(pl.multiple_of(half * part, part), part)
        inside = lax.broadcasted_iota(jnp.int32, (part, width), 0) + half * part
        attended = own_ref[rows, :]
        for ref, used in parts:
            limit = jnp.where(used > 0, asking * TILE, 0)
            attended = attended + jnp.where(inside < limit, ref[rows, :], 0.0)
        gated = row_norm(attended) * gate_ref[rows, :].astype(jnp.float32)
        mixed = jnp.dot(
            gated.astype(jnp.bfloat16), out_proj_ref[...], preferred_element_type=jnp.float32
        ) + event_ref[rows, :].astype(jnp.float32)
        for tile in range(tiles // 2):
            at = base + half * (tiles // 2) + tile
            here = users_ref[0, at]
            last = (at == count - 1) | (users_ref[0, jnp.minimum(at + 1, count - 1)] != here)
            limit = TILE - jnp.where(last, pad_ref[0, here], 0)
            kept = jnp.where(line < limit, mixed[tile * TILE : (tile + 1) * TILE], 0.0)
            out_ref[rows_at(half * (tiles // 2) + tile), :] = kept.astype(jnp.bfloat16)
        return carry

    lax.fori_loop(0, 2, finish, 0, unroll=True)


def scratch_of(height, width):
    tiles, pairs = height // TILE // 2, width // TILE
    return [
        pltpu.VMEM((pairs, tiles * 2 * TILE, TILE), jnp.bfloat16),
        pltpu.VMEM((pairs, tiles * 2 * TILE, TILE), jnp.bfloat16),
    ]


def earlier_part(kernel, name, flops, shard, users, block, w_keys_values, queries):
    height, width = queries.shape
    return pl.pallas_call(
        kernel,
        out_shape=jax.ShapeDtypeStruct((height, width), jnp.float32),
        in_specs=[smem()] * 2 + [vmem()] * 3,
        out_specs=vmem(),
        scratch_shapes=scratch_of(height, width),
        compiler_params=pltpu.CompilerParams(vmem_limit_bytes=24 * MIB),
        cost_estimate=pl.CostEstimate(flops=flops, bytes_accessed=10**5, transcendentals=0),
        name=name,
    )(shard, users, block, w_keys_values, queries)


def late(shard, users, pad, *arrays):
    height, width = arrays[2].shape
    return pl.pallas_call(
        late_kernel,
        out_shape=jax.ShapeDtypeStruct((height, width), jnp.bfloat16),
        in_specs=[smem()] * 3 + [vmem()] * len(arrays),
        out_specs=vmem(),
        scratch_shapes=[pltpu.VMEM((height, width), jnp.float32)] + scratch_of(height, width),
        compiler_params=pltpu.CompilerParams(vmem_limit_bytes=24 * MIB),
        cost_estimate=pl.CostEstimate(
            flops=8 * 10**9, bytes_accessed=10 * 10**6, transcendentals=4 * 10**6
        ),
        name="late",
    )(shard, users, pad, *arrays)


def on_device(item_ids, table, tile_user, tail_pad, w_proj, w_out):
    shards = lax.axis_size("seq")
    shard = lax.axis_index("seq").astype(jnp.int32).reshape(1, 1)
    events, normed, w_half = look_up(item_ids, table, w_proj)
    apart = [(i, i + 1 if i % 2 == 0 else i + 3) for i in range(shards)]
    mid = lax.ppermute(normed, "seq", [(i, i + 2) for i in range(shards - 2)])
    odd = lax.ppermute(normed, "seq", [(i, j) for i, j in apart if j < shards])
    gate, queries, total = own(shard, tile_user, normed, w_half)
    mid, queries = lax.optimization_barrier((mid, queries))
    swap = lax.ppermute(mid, "seq", [(i, i ^ 1) for i in range(shards)])
    w_keys_values = w_half[:, w_half.shape[1] // 2 :]
    given = (w_keys_values, queries)
    early = earlier_part(early_kernel, "early", 10**6, shard, tile_user, mid, *given)
    odd, early = lax.optimization_barrier((odd, early))
    middle = earlier_part(middle_kernel, "middle", 8 * 10**9, shard, tile_user, odd, *given)
    swap, middle = lax.optimization_barrier((swap, middle))
    mixed = late(
        shard,
        tile_user,
        tail_pad,
        swap,
        w_keys_values,
        queries,
        gate,
        total,
        early,
        middle,
        events,
        w_out,
    )
    return mixed[None]


def solution(mesh):
    in_specs = (P("batch", "seq"), P("batch", None), P("batch", None), P("batch", None), P(), P())
    out_specs = P("batch", "seq", None)
    return jax.shard_map(
        on_device, mesh=mesh, in_specs=in_specs, out_specs=out_specs, check_vma=False
    )
```

```python
import functools

import jax
import jax.numpy as jnp
from jax import lax
from jax.experimental import pallas as pl
from jax.experimental.pallas import tpu as pltpu
from jax.sharding import PartitionSpec as P

HEADS = 8
TILE = 128
REACH = 4
ROOM = 96
SLOTS = 128
MIB = 1 << 20


def vmem():
    return pl.BlockSpec(memory_space=pltpu.VMEM)


def smem():
    return pl.BlockSpec(memory_space=pltpu.SMEM)


def row_norm(values):
    center = values - jnp.mean(values, axis=-1, keepdims=True)
    spread = jnp.mean(center * center, axis=-1, keepdims=True)
    return center * lax.rsqrt(spread + 1e-05)


def half_silu(half):
    return half + half * jnp.tanh(half)


def owner_of(ids, entries, groups):
    owner = jnp.zeros_like(ids)
    for group in range(1, groups):
        owner = owner + jnp.where(ids >= group * entries, 1, 0)
    return owner


def route_kernel(groups, entries, row_ref, list_ref, slot_ref):
    height = row_ref.shape[1]
    ids = row_ref[...]
    lane = lax.broadcasted_iota(jnp.int32, (TILE, height), 1)
    line = lax.broadcasted_iota(jnp.int32, (TILE, height), 0)
    repeat = jnp.zeros((1, height), jnp.int32)
    columns = []
    for start in range(0, height, TILE):
        own_lane = jnp.where(line + start == lane, ids, 0).astype(jnp.float32)
        columns.append(jnp.sum(own_lane, axis=1, keepdims=True).astype(jnp.int32))
        same = (columns[-1] == ids[:, start:]) & (line[:, : height - start] < lane[:, : height - start])
        again = jnp.max(jnp.where(same, 1, 0), axis=0, keepdims=True)
        if start:
            again = jnp.concatenate([jnp.zeros((1, start), jnp.int32), again], axis=1)
        repeat = jnp.maximum(repeat, again)
    fresh = repeat == 0
    owner = owner_of(ids, entries, groups)
    lanes_of = lax.broadcasted_iota(jnp.int32, (groups, height), 0) == owner
    marked = jnp.where(lanes_of & fresh, 1.0, 0.0).astype(jnp.bfloat16)
    rank = jnp.zeros((groups, height), jnp.float32)
    for start in range(0, height, TILE):
        below = jnp.where(line + start < lane, 1.0, 0.0).astype(jnp.bfloat16)
        rank = rank + jnp.dot(
            marked[:, start : start + TILE], below, preferred_element_type=jnp.float32
        )
    place = jnp.sum(jnp.where(lanes_of, rank, 0.0), axis=0, keepdims=True)
    full = jnp.max(jnp.where(fresh, place, 0.0), axis=1, keepdims=True) >= ROOM
    slot = jnp.where(fresh, owner.astype(jnp.float32) * SLOTS + place, 0.0)
    wide = lax.broadcasted_iota(jnp.int32, (TILE, groups * SLOTS), 1)
    wanted = jnp.zeros((1, groups * SLOTS), jnp.int32)
    for start in range(0, height, TILE):
        column = columns[start // TILE]
        mine = jnp.sum(jnp.where(column == ids, slot, 0.0), axis=1, keepdims=True).astype(jnp.int32)
        holder = owner_of(column, entries, groups)
        slot_ref[pl.ds(start, TILE), :] = mine - holder * (SLOTS - ROOM)
        entry = column - holder * entries
        wanted = jnp.maximum(
            wanted, jnp.max(jnp.where(wide == mine, entry, 0), axis=0, keepdims=True)
        )
    place_of = lax.broadcasted_iota(jnp.int32, (1, groups * SLOTS), 1) & (SLOTS - 1)
    list_ref[...] = jnp.where(place_of >= ROOM, jnp.where(full, 1, 0), wanted)


def route(item_ids, groups, entries):
    height = item_ids.shape[1]
    return pl.pallas_call(
        functools.partial(route_kernel, groups, entries),
        out_shape=(
            jax.ShapeDtypeStruct((1, groups * SLOTS), jnp.int32),
            jax.ShapeDtypeStruct((height, 1), jnp.int32),
        ),
        in_specs=[vmem()],
        out_specs=(vmem(), vmem()),
        compiler_params=pltpu.CompilerParams(vmem_limit_bytes=16 * MIB),
        name="route",
    )(item_ids)


def expand_kernel(slot_ref, held_ref, event_ref, normed_ref, head_ref, tail_ref):
    rows = held_ref.shape[0]
    part = TILE
    wide = lax.broadcasted_iota(jnp.int32, (part, rows), 1)

    height = event_ref.shape[0]
    for start in range(0, height, part):
        place = pl.ds(start, part)
        pick = jnp.where(slot_ref[place, :] == wide, 1.0, 0.0).astype(jnp.bfloat16)
        events = jnp.dot(pick, held_ref[...], preferred_element_type=jnp.float32)
        normed = row_norm(events).astype(jnp.bfloat16)
        event_ref[place, :] = events.astype(jnp.bfloat16)
        normed_ref[place, :] = normed
        half_ref = head_ref if start < height // 2 else tail_ref
        half_ref[pl.ds(start % (height // 2), part), :] = normed


def expand(slot, held):
    height, width = slot.shape[0], held.shape[1]
    shape = jax.ShapeDtypeStruct((height, width), jnp.bfloat16)
    part = jax.ShapeDtypeStruct((height // 2, width), jnp.bfloat16)
    return pl.pallas_call(
        expand_kernel,
        out_shape=(shape, shape, part, part),
        in_specs=[vmem(), vmem()],
        out_specs=(vmem(), vmem(), vmem(), vmem()),
        compiler_params=pltpu.CompilerParams(vmem_limit_bytes=16 * MIB),
        name="expand",
    )(slot, held)


def look_up(item_ids, table, w_proj):
    groups = lax.axis_size("batch")
    height = item_ids.shape[1]
    entries, width = table.shape
    wanted, slot = route(item_ids, groups, entries)
    asked = lax.all_to_all(wanted.reshape(groups, SLOTS), "batch", 0, 0, tiled=True)
    crowded = jnp.max(asked[:, ROOM]) > 0
    picked = jnp.take(table, asked[:, :ROOM].reshape(-1), axis=0, mode="clip")
    held = lax.all_to_all(picked, "batch", 0, 0, tiled=True)
    held, w_half = lax.optimization_barrier((held, w_proj * jnp.bfloat16(0.5)))
    found = expand(slot, held)

    def whole():
        every = lax.all_to_all(
            jnp.broadcast_to(item_ids, (groups, height)), "batch", 0, 0, tiled=True
        )
        local = every.reshape(-1) - lax.axis_index("batch") * entries
        dense = jnp.take(table, local, axis=0, mode="clip")
        dense = lax.all_to_all(dense, "batch", 0, 0, tiled=True).reshape(groups, height, width)
        owner = item_ids[0] // entries
        rows = jnp.zeros((height, width), jnp.bfloat16)
        for group in range(groups):
            rows = jnp.where((owner == group)[:, None], dense[group], rows)
        normed = row_norm(rows.astype(jnp.float32)).astype(jnp.bfloat16)
        return rows, normed, normed[: height // 2], normed[height // 2 :]

    return *lax.cond(crowded, whole, lambda: found), w_half


def earlier_tiles(users_ref, tile, most):
    user = users_ref[0, tile]

    def look(back, count):
        at = tile - back
        here = (at >= 0) & (users_ref[0, jnp.maximum(at, 0)] == user)
        return count + jnp.where(here, 1, 0)

    return lax.fori_loop(1, most + 1, look, jnp.int32(0))


def rows_at(tile):
    return pl.ds(pl.multiple_of(tile * TILE, TILE), TILE)


def stack_heads(block, stack_ref, first_tile):
    lane = lax.broadcasted_iota(jnp.int32, (TILE, TILE), 1)
    heads = (lane < TILE // 2, lane >= TILE // 2)
    masks = [jnp.where(head, 1.0, 0.0).astype(jnp.bfloat16) for head in heads]
    for tile in range(block.shape[0] // TILE):
        for at in range(block.shape[1] // TILE):
            both = block[tile * TILE : (tile + 1) * TILE, at * TILE : (at + 1) * TILE]
            for which in range(2):
                place = pl.ds(pl.multiple_of((first_tile + tile) * 2 * TILE, TILE) + which * TILE, TILE)
                stack_ref[at, place, :] = both * masks[which]


def attend(query_ref, key_ref, value_ref, total_ref, rows, places, mask_ref=None, fresh=False):
    for at in range(key_ref.shape[0]):
        columns = slice(at * TILE, (at + 1) * TILE)
        half = lax.dot_general(
            query_ref[rows, columns],
            key_ref[at, places, :],
            (((1,), (1,)), ((), ())),
            preferred_element_type=jnp.float32,
        )
        weights = half_silu(half).astype(jnp.bfloat16)
        if mask_ref is not None:
            weights = weights * mask_ref[...]
        part = jnp.dot(weights, value_ref[at, places, :], preferred_element_type=jnp.float32)
        if fresh:
            total_ref[rows, columns] = part
        else:
            total_ref[rows, columns] += part


def project(normed, proj_ref, at, width):
    half = jnp.dot(
        normed, proj_ref[:, at * width : (at + 1) * width], preferred_element_type=jnp.float32
    )
    return half_silu(half).astype(jnp.bfloat16)


def own_kernel(
    shard_ref,
    users_ref,
    normed_ref,
    proj_ref,
    gate_ref,
    query_ref,
    total_ref,
    key_ref,
    value_ref,
    mask_ref,
):
    height, width = query_ref.shape
    tiles = height // TILE
    part = height // 2
    base = shard_ref[0, 0] * tiles

    def prepare(half, carry):
        rows = pl.ds(pl.multiple_of(half * part, part), part)
        normed = normed_ref[rows, :]
        gate_ref[rows, :] = project(normed, proj_ref, 0, width)
        query_ref[rows, :] = project(normed, proj_ref, 1, width) * jnp.bfloat16(0.5)
        stack_heads(project(normed, proj_ref, 2, width), key_ref, half * (tiles // 2))
        stack_heads(project(normed, proj_ref, 3, width), value_ref, half * (tiles // 2))
        return carry

    lax.fori_loop(0, 2, prepare, 0)

    line = lax.broadcasted_iota(jnp.int32, (TILE, 2 * part), 0)
    lane = lax.broadcasted_iota(jnp.int32, (TILE, 2 * part), 1)
    key_row = lax.shift_right_logical(lane, 8) * TILE + (lane & (TILE - 1))

    def block(query_half, key_half, fresh):
        def look(tile, carry):
            at = query_half * (tiles // 2) + tile
            first = at - earlier_tiles(users_ref, base + at, tiles - 1)
            least = (first - key_half * (tiles // 2)) * TILE
            most = line + (tile + (query_half - key_half) * (tiles // 2)) * TILE
            seen = (key_row >= least) & (key_row <= most)
            mask_ref[rows_at(tile), :] = jnp.where(seen, 1.0, 0.0).astype(jnp.bfloat16)
            return carry

        lax.fori_loop(0, tiles // 2, look, 0)
        attend(
            query_ref,
            key_ref,
            value_ref,
            total_ref,
            pl.ds(pl.multiple_of(query_half * part, part), part),
            pl.ds(pl.multiple_of(key_half * 2 * part, part), 2 * part),
            mask_ref,
            fresh,
        )

    def same(half, carry):
        block(half, half, True)
        return carry

    lax.fori_loop(0, 2, same, 0)
    middle = base + tiles // 2

    @pl.when(users_ref[0, middle] == users_ref[0, middle - 1])
    def _():
        block(1, 0, False)


def own(shard, users, normed, w_proj):
    height, width = normed.shape
    tiles, pairs = height // TILE, width // TILE
    return pl.pallas_call(
        own_kernel,
        out_shape=(
            jax.ShapeDtypeStruct((height, width), jnp.bfloat16),
            jax.ShapeDtypeStruct((height, width), jnp.bfloat16),
            jax.ShapeDtypeStruct((height, width), jnp.float32),
        ),
        in_specs=[smem(), smem(), vmem(), vmem()],
        out_specs=(vmem(), vmem(), vmem()),
        scratch_shapes=[
            pltpu.VMEM((pairs, tiles * 2 * TILE, TILE), jnp.bfloat16),
            pltpu.VMEM((pairs, tiles * 2 * TILE, TILE), jnp.bfloat16),
            pltpu.VMEM((height // 2, height), jnp.bfloat16),
        ],
        compiler_params=pltpu.CompilerParams(vmem_limit_bytes=24 * MIB),
        cost_estimate=pl.CostEstimate(flops=10**6, bytes_accessed=10**5, transcendentals=0),
        name="own",
    )(shard, users, normed, w_proj)


def add_half(
    normed, half, begin, asking, proj_ref, query_ref, total_ref, key_ref, value_ref
):
    part, width = normed.shape
    line = lax.broadcasted_iota(jnp.int32, (part, width), 0) + half * part
    values = project(normed, proj_ref, 1, width)
    values = jnp.where(line >= begin, values.astype(jnp.float32), 0.0)
    stack_heads(project(normed, proj_ref, 0, width), key_ref, 0)
    stack_heads(values.astype(jnp.bfloat16), value_ref, 0)

    def query(at, carry):
        attend(
            query_ref,
            key_ref,
            value_ref,
            total_ref,
            pl.ds(pl.multiple_of(at * part, part), part),
            pl.ds(0, 2 * part),
        )
        return carry

    lax.fori_loop(0, jnp.where(asking * TILE > part, 2, 1), query, 0)


def add_earlier(
    block_of, distance, needed, asking, proj_ref, query_ref, total_ref, key_ref, value_ref
):
    height = query_ref.shape[0]
    part = height // 2
    used = used_of(needed, distance, height // TILE)

    @pl.when(used > 0)
    def _():
        total_ref[...] = jnp.zeros_like(total_ref)

    def each(half, carry):
        add_half(
            block_of(half),
            half,
            height - used * TILE,
            asking,
            proj_ref,
            query_ref,
            total_ref,
            key_ref,
            value_ref,
        )
        return carry

    lax.fori_loop(jnp.where(used * TILE > part, 0, 1), jnp.where(used > 0, 2, 0), each, 0)


def used_of(needed, distance, tiles):
    return jnp.clip(needed - tiles * (distance - 1), 0, tiles)


def reach(shard_ref, users_ref, tiles):
    base = shard_ref[0, 0] * tiles
    needed = earlier_tiles(users_ref, base, (REACH - 1) * tiles)
    asking = jnp.int32(0)
    for tile in range(tiles):
        asking = asking + jnp.where(users_ref[0, base + tile] == users_ref[0, base], 1, 0)
    return base, needed, asking


def early_kernel(
    half,
    shard_ref,
    users_ref,
    proj_ref,
    query_ref,
    block_ref,
    total_ref,
    key_ref,
    value_ref,
):
    height = query_ref.shape[0]
    _, needed, asking = reach(shard_ref, users_ref, height // TILE)
    used = used_of(needed, 2, height // TILE)

    @pl.when(used * TILE > height // 2 * (1 - half))
    def _():
        total_ref[...] = jnp.zeros_like(total_ref)
        add_half(
            block_ref[...],
            half,
            height - used * TILE,
            asking,
            proj_ref,
            query_ref,
            total_ref,
            key_ref,
            value_ref,
        )


def middle_kernel(
    shard_ref,
    users_ref,
    proj_ref,
    query_ref,
    head_ref,
    tail_ref,
    total_ref,
    key_ref,
    value_ref,
):
    def block_of(half):
        return jnp.where(half == 0, head_ref[...], tail_ref[...])

    _, needed, asking = reach(shard_ref, users_ref, query_ref.shape[0] // TILE)
    add_earlier(
        block_of,
        3 - 2 * lax.rem(shard_ref[0, 0], 2),
        needed,
        asking,
        proj_ref,
        query_ref,
        total_ref,
        key_ref,
        value_ref,
    )


def late_kernel(
    shard_ref,
    users_ref,
    pad_ref,
    head_ref,
    tail_ref,
    proj_ref,
    query_ref,
    gate_ref,
    own_ref,
    early_tail_ref,
    early_head_ref,
    middle_ref,
    event_ref,
    out_proj_ref,
    out_ref,
    total_ref,
    key_ref,
    value_ref,
):
    height, width = query_ref.shape
    tiles = height // TILE
    count = users_ref.shape[1]
    base, needed, asking = reach(shard_ref, users_ref, tiles)
    core = lax.rem(shard_ref[0, 0], 2)

    def block_of(half):
        return jnp.where(half == 0, head_ref[...], tail_ref[...])

    add_earlier(
        block_of,
        1 + 2 * core,
        needed,
        asking,
        proj_ref,
        query_ref,
        total_ref,
        key_ref,
        value_ref,
    )
    parts = (
        (early_tail_ref, used_of(needed, 2, tiles)),
        (early_head_ref, used_of(needed, 2, tiles) - tiles // 2),
        (middle_ref, used_of(needed, 3 - 2 * core, tiles)),
        (total_ref, used_of(needed, 1 + 2 * core, tiles)),
    )
    part = height // 2

    line = lax.broadcasted_iota(jnp.int32, (TILE, width), 0)

    def finish(half, carry):
        rows = pl.ds(pl.multiple_of(half * part, part), part)
        inside = lax.broadcasted_iota(jnp.int32, (part, width), 0) + half * part
        attended = own_ref[rows, :]
        for ref, used in parts:
            limit = jnp.where(used > 0, asking * TILE, 0)
            attended = attended + jnp.where(inside < limit, ref[rows, :], 0.0)
        gated = row_norm(attended) * gate_ref[rows, :].astype(jnp.float32)
        mixed = jnp.dot(
            gated.astype(jnp.bfloat16), out_proj_ref[...], preferred_element_type=jnp.float32
        ) + event_ref[rows, :].astype(jnp.float32)
        for tile in range(tiles // 2):
            at = base + half * (tiles // 2) + tile
            here = users_ref[0, at]
            last = (at == count - 1) | (users_ref[0, jnp.minimum(at + 1, count - 1)] != here)
            limit = TILE - jnp.where(last, pad_ref[0, here], 0)
            kept = jnp.where(line < limit, mixed[tile * TILE : (tile + 1) * TILE], 0.0)
            out_ref[rows_at(half * (tiles // 2) + tile), :] = kept.astype(jnp.bfloat16)
        return carry

    lax.fori_loop(0, 2, finish, 0, unroll=True)


def scratch_of(height, width):
    tiles, pairs = height // TILE // 2, width // TILE
    return [
        pltpu.VMEM((pairs, tiles * 2 * TILE, TILE), jnp.bfloat16),
        pltpu.VMEM((pairs, tiles * 2 * TILE, TILE), jnp.bfloat16),
    ]


def earlier_part(kernel, name, flops, shard, users, w_keys_values, queries, *blocks):
    height, width = queries.shape
    return pl.pallas_call(
        kernel,
        out_shape=jax.ShapeDtypeStruct((height, width), jnp.float32),
        in_specs=[smem()] * 2 + [vmem()] * (2 + len(blocks)),
        out_specs=vmem(),
        scratch_shapes=scratch_of(height, width),
        compiler_params=pltpu.CompilerParams(vmem_limit_bytes=24 * MIB),
        cost_estimate=pl.CostEstimate(flops=flops, bytes_accessed=10**5, transcendentals=0),
        name=name,
    )(shard, users, w_keys_values, queries, *blocks)


def late(shard, users, pad, *arrays):
    height, width = arrays[3].shape
    return pl.pallas_call(
        late_kernel,
        out_shape=jax.ShapeDtypeStruct((height, width), jnp.bfloat16),
        in_specs=[smem()] * 3 + [vmem()] * len(arrays),
        out_specs=vmem(),
        scratch_shapes=[pltpu.VMEM((height, width), jnp.float32)] + scratch_of(height, width),
        compiler_params=pltpu.CompilerParams(vmem_limit_bytes=24 * MIB),
        cost_estimate=pl.CostEstimate(
            flops=8 * 10**9, bytes_accessed=10 * 10**6, transcendentals=4 * 10**6
        ),
        name="late",
    )(shard, users, pad, *arrays)


def on_device(item_ids, table, tile_user, tail_pad, w_proj, w_out):
    shards = lax.axis_size("seq")
    shard = lax.axis_index("seq").astype(jnp.int32).reshape(1, 1)
    events, normed, head, tail, w_half = look_up(item_ids, table, w_proj)
    apart = [(i, i + 1 if i % 2 == 0 else i + 3) for i in range(shards)]
    ahead = [(i, i + 2) for i in range(shards - 2)]
    cores = [(i, i ^ 1) for i in range(shards)]
    mid_tail = lax.ppermute(tail, "seq", ahead)
    mid_head = lax.ppermute(head, "seq", ahead)
    apart = [(i, j) for i, j in apart if j < shards]
    odd_tail = lax.ppermute(tail, "seq", apart)
    odd_head = lax.ppermute(head, "seq", apart)
    gate, queries, total = own(shard, tile_user, normed, w_half)
    w_keys_values = w_half[:, w_half.shape[1] // 2 :]

    def part_of(kernel, name, flops, *blocks):
        return earlier_part(kernel, name, flops, shard, tile_user, w_keys_values, queries, *blocks)

    mid_tail, queries = lax.optimization_barrier((mid_tail, queries))
    swap_tail = lax.ppermute(mid_tail, "seq", cores)
    early_tail = part_of(functools.partial(early_kernel, 1), "early_tail", 10**6, mid_tail)
    mid_head, early_tail = lax.optimization_barrier((mid_head, early_tail))
    swap_head = lax.ppermute(mid_head, "seq", cores)
    early_head = part_of(functools.partial(early_kernel, 0), "early_head", 10**6, mid_head)
    odd_head, odd_tail, early_head = lax.optimization_barrier((odd_head, odd_tail, early_head))
    middle = part_of(middle_kernel, "middle", 8 * 10**9, odd_head, odd_tail)
    swap_head, swap_tail, middle = lax.optimization_barrier((swap_head, swap_tail, middle))
    mixed = late(
        shard,
        tile_user,
        tail_pad,
        swap_head,
        swap_tail,
        w_keys_values,
        queries,
        gate,
        total,
        early_tail,
        early_head,
        middle,
        events,
        w_out,
    )
    return mixed[None]


def solution(mesh):
    in_specs = (P("batch", "seq"), P("batch", None), P("batch", None), P("batch", None), P(), P())
    out_specs = P("batch", "seq", None)
    return jax.shard_map(
        on_device, mesh=mesh, in_specs=in_specs, out_specs=out_specs, check_vma=False
    )
```

```python
import functools

import jax
import jax.numpy as jnp
from jax import lax
from jax.experimental import pallas as pl
from jax.experimental.pallas import tpu as pltpu
from jax.sharding import PartitionSpec as P

HEADS = 8
TILE = 128
REACH = 4
ROOM = 96
SLOTS = 128
MIB = 1 << 20


def vmem():
    return pl.BlockSpec(memory_space=pltpu.VMEM)


def smem():
    return pl.BlockSpec(memory_space=pltpu.SMEM)


def row_norm(values):
    center = values - jnp.mean(values, axis=-1, keepdims=True)
    spread = jnp.mean(center * center, axis=-1, keepdims=True)
    return center * lax.rsqrt(spread + 1e-05)


def half_silu(half):
    return half + half * jnp.tanh(half)


def owner_of(ids, entries, groups):
    owner = jnp.zeros_like(ids)
    for group in range(1, groups):
        owner = owner + jnp.where(ids >= group * entries, 1, 0)
    return owner


def route_kernel(groups, entries, row_ref, list_ref, slot_ref):
    height = row_ref.shape[1]
    ids = row_ref[...]
    lane = lax.broadcasted_iota(jnp.int32, (TILE, height), 1)
    line = lax.broadcasted_iota(jnp.int32, (TILE, height), 0)
    repeat = jnp.zeros((1, height), jnp.int32)
    columns = []
    for start in range(0, height, TILE):
        own_lane = jnp.where(line + start == lane, ids, 0).astype(jnp.float32)
        columns.append(jnp.sum(own_lane, axis=1, keepdims=True).astype(jnp.int32))
        same = (columns[-1] == ids[:, start:]) & (line[:, : height - start] < lane[:, : height - start])
        again = jnp.max(jnp.where(same, 1, 0), axis=0, keepdims=True)
        if start:
            again = jnp.concatenate([jnp.zeros((1, start), jnp.int32), again], axis=1)
        repeat = jnp.maximum(repeat, again)
    fresh = repeat == 0
    owner = owner_of(ids, entries, groups)
    lanes_of = lax.broadcasted_iota(jnp.int32, (groups, height), 0) == owner
    marked = jnp.where(lanes_of & fresh, 1.0, 0.0).astype(jnp.bfloat16)
    rank = jnp.zeros((groups, height), jnp.float32)
    for start in range(0, height, TILE):
        below = jnp.where(line + start < lane, 1.0, 0.0).astype(jnp.bfloat16)
        rank = rank + jnp.dot(
            marked[:, start : start + TILE], below, preferred_element_type=jnp.float32
        )
    place = jnp.sum(jnp.where(lanes_of, rank, 0.0), axis=0, keepdims=True)
    full = jnp.max(jnp.where(fresh, place, 0.0), axis=1, keepdims=True) >= ROOM
    slot = jnp.where(fresh, owner.astype(jnp.float32) * SLOTS + place, 0.0)
    wide = lax.broadcasted_iota(jnp.int32, (TILE, groups * SLOTS), 1)
    wanted = jnp.zeros((1, groups * SLOTS), jnp.int32)
    for start in range(0, height, TILE):
        column = columns[start // TILE]
        mine = jnp.sum(jnp.where(column == ids, slot, 0.0), axis=1, keepdims=True).astype(jnp.int32)
        holder = owner_of(column, entries, groups)
        slot_ref[pl.ds(start, TILE), :] = mine - holder * (SLOTS - ROOM)
        entry = column - holder * entries
        wanted = jnp.maximum(
            wanted, jnp.max(jnp.where(wide == mine, entry, 0), axis=0, keepdims=True)
        )
    place_of = lax.broadcasted_iota(jnp.int32, (1, groups * SLOTS), 1) & (SLOTS - 1)
    list_ref[...] = jnp.where(place_of >= ROOM, jnp.where(full, 1, 0), wanted)


def route(item_ids, groups, entries):
    height = item_ids.shape[1]
    return pl.pallas_call(
        functools.partial(route_kernel, groups, entries),
        out_shape=(
            jax.ShapeDtypeStruct((1, groups * SLOTS), jnp.int32),
            jax.ShapeDtypeStruct((height, 1), jnp.int32),
        ),
        in_specs=[vmem()],
        out_specs=(vmem(), vmem()),
        compiler_params=pltpu.CompilerParams(vmem_limit_bytes=16 * MIB),
        name="route",
    )(item_ids)


def expand_kernel(slot_ref, held_ref, event_ref, head_ref, tail_ref):
    rows = held_ref.shape[0]
    part = TILE
    wide = lax.broadcasted_iota(jnp.int32, (part, rows), 1)

    height = event_ref.shape[0]
    for start in range(0, height, part):
        place = pl.ds(start, part)
        pick = jnp.where(slot_ref[place, :] == wide, 1.0, 0.0).astype(jnp.bfloat16)
        events = jnp.dot(pick, held_ref[...], preferred_element_type=jnp.float32)
        normed = row_norm(events).astype(jnp.bfloat16)
        event_ref[place, :] = events.astype(jnp.bfloat16)
        half_ref = head_ref if start < height // 2 else tail_ref
        half_ref[pl.ds(start % (height // 2), part), :] = normed


def expand(slot, held):
    height, width = slot.shape[0], held.shape[1]
    shape = jax.ShapeDtypeStruct((height, width), jnp.bfloat16)
    part = jax.ShapeDtypeStruct((height // 2, width), jnp.bfloat16)
    return pl.pallas_call(
        expand_kernel,
        out_shape=(shape, part, part),
        in_specs=[vmem(), vmem()],
        out_specs=(vmem(), vmem(), vmem()),
        compiler_params=pltpu.CompilerParams(vmem_limit_bytes=16 * MIB),
        name="expand",
    )(slot, held)


def look_up(item_ids, table, w_proj):
    groups = lax.axis_size("batch")
    height = item_ids.shape[1]
    entries, width = table.shape
    wanted, slot = route(item_ids, groups, entries)
    asked = lax.all_to_all(wanted.reshape(groups, SLOTS), "batch", 0, 0, tiled=True)
    crowded = jnp.max(asked[:, ROOM]) > 0
    picked = jnp.take(table, asked[:, :ROOM].reshape(-1), axis=0, mode="clip")
    held = lax.all_to_all(picked, "batch", 0, 0, tiled=True)
    held, w_half = lax.optimization_barrier((held, w_proj * jnp.bfloat16(0.5)))
    found = expand(slot, held)

    def whole():
        every = lax.all_to_all(
            jnp.broadcast_to(item_ids, (groups, height)), "batch", 0, 0, tiled=True
        )
        local = every.reshape(-1) - lax.axis_index("batch") * entries
        dense = jnp.take(table, local, axis=0, mode="clip")
        dense = lax.all_to_all(dense, "batch", 0, 0, tiled=True).reshape(groups, height, width)
        owner = item_ids[0] // entries
        rows = jnp.zeros((height, width), jnp.bfloat16)
        for group in range(groups):
            rows = jnp.where((owner == group)[:, None], dense[group], rows)
        normed = row_norm(rows.astype(jnp.float32)).astype(jnp.bfloat16)
        return rows, normed[: height // 2], normed[height // 2 :]

    return *lax.cond(crowded, whole, lambda: found), w_half


def earlier_tiles(users_ref, tile, most):
    user = users_ref[0, tile]

    def look(back, count):
        at = tile - back
        here = (at >= 0) & (users_ref[0, jnp.maximum(at, 0)] == user)
        return count + jnp.where(here, 1, 0)

    return lax.fori_loop(1, most + 1, look, jnp.int32(0))


def rows_at(tile):
    return pl.ds(pl.multiple_of(tile * TILE, TILE), TILE)


def stack_heads(block, stack_ref, first_tile):
    lane = lax.broadcasted_iota(jnp.int32, (TILE, TILE), 1)
    heads = (lane < TILE // 2, lane >= TILE // 2)
    masks = [jnp.where(head, 1.0, 0.0).astype(jnp.bfloat16) for head in heads]
    for tile in range(block.shape[0] // TILE):
        for at in range(block.shape[1] // TILE):
            both = block[tile * TILE : (tile + 1) * TILE, at * TILE : (at + 1) * TILE]
            for which in range(2):
                place = pl.ds(pl.multiple_of((first_tile + tile) * 2 * TILE, TILE) + which * TILE, TILE)
                stack_ref[at, place, :] = both * masks[which]


def attend(query_ref, key_ref, value_ref, total_ref, rows, places, mask_ref=None, fresh=False):
    for at in range(key_ref.shape[0]):
        columns = slice(at * TILE, (at + 1) * TILE)
        half = lax.dot_general(
            query_ref[rows, columns],
            key_ref[at, places, :],
            (((1,), (1,)), ((), ())),
            preferred_element_type=jnp.float32,
        )
        weights = half_silu(half).astype(jnp.bfloat16)
        if mask_ref is not None:
            weights = weights * mask_ref[...]
        part = jnp.dot(weights, value_ref[at, places, :], preferred_element_type=jnp.float32)
        if fresh:
            total_ref[rows, columns] = part
        else:
            total_ref[rows, columns] += part


def project(normed, proj_ref, at, width):
    half = jnp.dot(
        normed, proj_ref[:, at * width : (at + 1) * width], preferred_element_type=jnp.float32
    )
    return half_silu(half).astype(jnp.bfloat16)


def own_kernel(
    shard_ref,
    users_ref,
    head_ref,
    tail_ref,
    proj_ref,
    gate_ref,
    query_ref,
    total_ref,
    key_ref,
    value_ref,
    mask_ref,
):
    height, width = query_ref.shape
    tiles = height // TILE
    part = height // 2
    base = shard_ref[0, 0] * tiles

    def prepare(half, carry):
        rows = pl.ds(pl.multiple_of(half * part, part), part)
        normed = jnp.where(half == 0, head_ref[...], tail_ref[...])
        gate_ref[rows, :] = project(normed, proj_ref, 0, width)
        query_ref[rows, :] = project(normed, proj_ref, 1, width) * jnp.bfloat16(0.5)
        stack_heads(project(normed, proj_ref, 2, width), key_ref, half * (tiles // 2))
        stack_heads(project(normed, proj_ref, 3, width), value_ref, half * (tiles // 2))
        return carry

    lax.fori_loop(0, 2, prepare, 0)

    line = lax.broadcasted_iota(jnp.int32, (TILE, 2 * part), 0)
    lane = lax.broadcasted_iota(jnp.int32, (TILE, 2 * part), 1)
    key_row = lax.shift_right_logical(lane, 8) * TILE + (lane & (TILE - 1))

    def block(query_half, key_half, fresh):
        def look(tile, carry):
            at = query_half * (tiles // 2) + tile
            first = at - earlier_tiles(users_ref, base + at, tiles - 1)
            least = (first - key_half * (tiles // 2)) * TILE
            most = line + (tile + (query_half - key_half) * (tiles // 2)) * TILE
            seen = (key_row >= least) & (key_row <= most)
            mask_ref[rows_at(tile), :] = jnp.where(seen, 1.0, 0.0).astype(jnp.bfloat16)
            return carry

        lax.fori_loop(0, tiles // 2, look, 0)
        attend(
            query_ref,
            key_ref,
            value_ref,
            total_ref,
            pl.ds(pl.multiple_of(query_half * part, part), part),
            pl.ds(pl.multiple_of(key_half * 2 * part, part), 2 * part),
            mask_ref,
            fresh,
        )

    def same(half, carry):
        block(half, half, True)
        return carry

    lax.fori_loop(0, 2, same, 0)
    middle = base + tiles // 2

    @pl.when(users_ref[0, middle] == users_ref[0, middle - 1])
    def _():
        block(1, 0, False)


def own(shard, users, head, tail, w_proj):
    height, width = 2 * head.shape[0], head.shape[1]
    tiles, pairs = height // TILE, width // TILE
    return pl.pallas_call(
        own_kernel,
        out_shape=(
            jax.ShapeDtypeStruct((height, width), jnp.bfloat16),
            jax.ShapeDtypeStruct((height, width), jnp.bfloat16),
            jax.ShapeDtypeStruct((height, width), jnp.float32),
        ),
        in_specs=[smem(), smem(), vmem(), vmem(), vmem()],
        out_specs=(vmem(), vmem(), vmem()),
        scratch_shapes=[
            pltpu.VMEM((pairs, tiles * 2 * TILE, TILE), jnp.bfloat16),
            pltpu.VMEM((pairs, tiles * 2 * TILE, TILE), jnp.bfloat16),
            pltpu.VMEM((height // 2, height), jnp.bfloat16),
        ],
        compiler_params=pltpu.CompilerParams(vmem_limit_bytes=24 * MIB),
        cost_estimate=pl.CostEstimate(flops=10**6, bytes_accessed=10**5, transcendentals=0),
        name="own",
    )(shard, users, head, tail, w_proj)


def add_half(
    normed, half, begin, asking, proj_ref, query_ref, total_ref, key_ref, value_ref
):
    part, width = normed.shape
    line = lax.broadcasted_iota(jnp.int32, (part, width), 0) + half * part
    values = project(normed, proj_ref, 1, width)
    values = jnp.where(line >= begin, values.astype(jnp.float32), 0.0)
    stack_heads(project(normed, proj_ref, 0, width), key_ref, 0)
    stack_heads(values.astype(jnp.bfloat16), value_ref, 0)

    def query(at, carry):
        attend(
            query_ref,
            key_ref,
            value_ref,
            total_ref,
            pl.ds(pl.multiple_of(at * part, part), part),
            pl.ds(0, 2 * part),
        )
        return carry

    lax.fori_loop(0, jnp.where(asking * TILE > part, 2, 1), query, 0)


def add_earlier(
    block_of, distance, needed, asking, proj_ref, query_ref, total_ref, key_ref, value_ref
):
    height = query_ref.shape[0]
    part = height // 2
    used = used_of(needed, distance, height // TILE)

    @pl.when(used > 0)
    def _():
        total_ref[...] = jnp.zeros_like(total_ref)

    def each(half, carry):
        add_half(
            block_of(half),
            half,
            height - used * TILE,
            asking,
            proj_ref,
            query_ref,
            total_ref,
            key_ref,
            value_ref,
        )
        return carry

    lax.fori_loop(jnp.where(used * TILE > part, 0, 1), jnp.where(used > 0, 2, 0), each, 0)


def used_of(needed, distance, tiles):
    return jnp.clip(needed - tiles * (distance - 1), 0, tiles)


def reach(shard_ref, users_ref, tiles):
    base = shard_ref[0, 0] * tiles
    needed = earlier_tiles(users_ref, base, (REACH - 1) * tiles)
    asking = jnp.int32(0)
    for tile in range(tiles):
        asking = asking + jnp.where(users_ref[0, base + tile] == users_ref[0, base], 1, 0)
    return base, needed, asking


def early_kernel(
    half,
    shard_ref,
    users_ref,
    proj_ref,
    query_ref,
    block_ref,
    total_ref,
    key_ref,
    value_ref,
):
    height = query_ref.shape[0]
    _, needed, asking = reach(shard_ref, users_ref, height // TILE)
    used = used_of(needed, 2, height // TILE)

    @pl.when(used * TILE > height // 2 * (1 - half))
    def _():
        total_ref[...] = jnp.zeros_like(total_ref)
        add_half(
            block_ref[...],
            half,
            height - used * TILE,
            asking,
            proj_ref,
            query_ref,
            total_ref,
            key_ref,
            value_ref,
        )


def middle_kernel(
    shard_ref,
    users_ref,
    proj_ref,
    query_ref,
    head_ref,
    tail_ref,
    total_ref,
    key_ref,
    value_ref,
):
    def block_of(half):
        return jnp.where(half == 0, head_ref[...], tail_ref[...])

    _, needed, asking = reach(shard_ref, users_ref, query_ref.shape[0] // TILE)
    add_earlier(
        block_of,
        3 - 2 * lax.rem(shard_ref[0, 0], 2),
        needed,
        asking,
        proj_ref,
        query_ref,
        total_ref,
        key_ref,
        value_ref,
    )


def late_kernel(
    shard_ref,
    users_ref,
    pad_ref,
    head_ref,
    tail_ref,
    proj_ref,
    query_ref,
    gate_ref,
    own_ref,
    early_tail_ref,
    early_head_ref,
    middle_ref,
    event_ref,
    out_proj_ref,
    out_ref,
    total_ref,
    key_ref,
    value_ref,
):
    height, width = query_ref.shape
    tiles = height // TILE
    count = users_ref.shape[1]
    base, needed, asking = reach(shard_ref, users_ref, tiles)
    core = lax.rem(shard_ref[0, 0], 2)

    def block_of(half):
        return jnp.where(half == 0, head_ref[...], tail_ref[...])

    add_earlier(
        block_of,
        1 + 2 * core,
        needed,
        asking,
        proj_ref,
        query_ref,
        total_ref,
        key_ref,
        value_ref,
    )
    parts = (
        (early_tail_ref, used_of(needed, 2, tiles)),
        (early_head_ref, used_of(needed, 2, tiles) - tiles // 2),
        (middle_ref, used_of(needed, 3 - 2 * core, tiles)),
        (total_ref, used_of(needed, 1 + 2 * core, tiles)),
    )
    part = height // 2

    line = lax.broadcasted_iota(jnp.int32, (TILE, width), 0)

    def finish(half, carry):
        rows = pl.ds(pl.multiple_of(half * part, part), part)
        inside = lax.broadcasted_iota(jnp.int32, (part, width), 0) + half * part
        attended = own_ref[rows, :]
        for ref, used in parts:
            limit = jnp.where(used > 0, asking * TILE, 0)
            attended = attended + jnp.where(inside < limit, ref[rows, :], 0.0)
        gated = row_norm(attended) * gate_ref[rows, :].astype(jnp.float32)
        mixed = jnp.dot(
            gated.astype(jnp.bfloat16), out_proj_ref[...], preferred_element_type=jnp.float32
        ) + event_ref[rows, :].astype(jnp.float32)
        for tile in range(tiles // 2):
            at = base + half * (tiles // 2) + tile
            here = users_ref[0, at]
            last = (at == count - 1) | (users_ref[0, jnp.minimum(at + 1, count - 1)] != here)
            limit = TILE - jnp.where(last, pad_ref[0, here], 0)
            kept = jnp.where(line < limit, mixed[tile * TILE : (tile + 1) * TILE], 0.0)
            out_ref[rows_at(half * (tiles // 2) + tile), :] = kept.astype(jnp.bfloat16)
        return carry

    lax.fori_loop(0, 2, finish, 0, unroll=True)


def scratch_of(height, width):
    tiles, pairs = height // TILE // 2, width // TILE
    return [
        pltpu.VMEM((pairs, tiles * 2 * TILE, TILE), jnp.bfloat16),
        pltpu.VMEM((pairs, tiles * 2 * TILE, TILE), jnp.bfloat16),
    ]


def earlier_part(kernel, name, flops, shard, users, w_keys_values, queries, *blocks):
    height, width = queries.shape
    return pl.pallas_call(
        kernel,
        out_shape=jax.ShapeDtypeStruct((height, width), jnp.float32),
        in_specs=[smem()] * 2 + [vmem()] * (2 + len(blocks)),
        out_specs=vmem(),
        scratch_shapes=scratch_of(height, width),
        compiler_params=pltpu.CompilerParams(vmem_limit_bytes=24 * MIB),
        cost_estimate=pl.CostEstimate(flops=flops, bytes_accessed=10**5, transcendentals=0),
        name=name,
    )(shard, users, w_keys_values, queries, *blocks)


def late(shard, users, pad, *arrays):
    height, width = arrays[3].shape
    return pl.pallas_call(
        late_kernel,
        out_shape=jax.ShapeDtypeStruct((height, width), jnp.bfloat16),
        in_specs=[smem()] * 3 + [vmem()] * len(arrays),
        out_specs=vmem(),
        scratch_shapes=[pltpu.VMEM((height, width), jnp.float32)] + scratch_of(height, width),
        compiler_params=pltpu.CompilerParams(vmem_limit_bytes=24 * MIB),
        cost_estimate=pl.CostEstimate(
            flops=8 * 10**9, bytes_accessed=10 * 10**6, transcendentals=4 * 10**6
        ),
        name="late",
    )(shard, users, pad, *arrays)


def on_device(item_ids, table, tile_user, tail_pad, w_proj, w_out):
    shards = lax.axis_size("seq")
    shard = lax.axis_index("seq").astype(jnp.int32).reshape(1, 1)
    events, head, tail, w_half = look_up(item_ids, table, w_proj)
    apart = [(i, i + 1 if i % 2 == 0 else i + 3) for i in range(shards)]
    ahead = [(i, i + 2) for i in range(shards - 2)]
    cores = [(i, i ^ 1) for i in range(shards)]
    mid_tail = lax.ppermute(tail, "seq", ahead)
    mid_head = lax.ppermute(head, "seq", ahead)
    apart = [(i, j) for i, j in apart if j < shards]
    odd_tail = lax.ppermute(tail, "seq", apart)
    odd_head = lax.ppermute(head, "seq", apart)
    gate, queries, total = own(shard, tile_user, head, tail, w_half)
    w_keys_values = w_half[:, w_half.shape[1] // 2 :]

    def part_of(kernel, name, flops, *blocks):
        return earlier_part(kernel, name, flops, shard, tile_user, w_keys_values, queries, *blocks)

    mid_tail, queries = lax.optimization_barrier((mid_tail, queries))
    swap_tail = lax.ppermute(mid_tail, "seq", cores)
    early_tail = part_of(functools.partial(early_kernel, 1), "early_tail", 10**6, mid_tail)
    mid_head, early_tail = lax.optimization_barrier((mid_head, early_tail))
    swap_head = lax.ppermute(mid_head, "seq", cores)
    early_head = part_of(functools.partial(early_kernel, 0), "early_head", 10**6, mid_head)
    odd_head, odd_tail, early_head = lax.optimization_barrier((odd_head, odd_tail, early_head))
    middle = part_of(middle_kernel, "middle", 8 * 10**9, odd_head, odd_tail)
    swap_head, swap_tail, middle = lax.optimization_barrier((swap_head, swap_tail, middle))
    mixed = late(
        shard,
        tile_user,
        tail_pad,
        swap_head,
        swap_tail,
        w_keys_values,
        queries,
        gate,
        total,
        early_tail,
        early_head,
        middle,
        events,
        w_out,
    )
    return mixed[None]


def solution(mesh):
    in_specs = (P("batch", "seq"), P("batch", None), P("batch", None), P("batch", None), P(), P())
    out_specs = P("batch", "seq", None)
    return jax.shard_map(
        on_device, mesh=mesh, in_specs=in_specs, out_specs=out_specs, check_vma=False
    )
```

```python
import functools

import jax
import jax.numpy as jnp
from jax import lax
from jax.experimental import pallas as pl
from jax.experimental.pallas import tpu as pltpu
from jax.sharding import PartitionSpec as P

HEADS = 8
TILE = 128
REACH = 4
ROOM = 96
SLOTS = 128
MIB = 1 << 20


def vmem():
    return pl.BlockSpec(memory_space=pltpu.VMEM)


def smem():
    return pl.BlockSpec(memory_space=pltpu.SMEM)


def row_norm(values):
    center = values - jnp.mean(values, axis=-1, keepdims=True)
    spread = jnp.mean(center * center, axis=-1, keepdims=True)
    return center * lax.rsqrt(spread + 1e-05)


def half_silu(half):
    return half + half * jnp.tanh(half)


def owner_of(ids, entries, groups):
    owner = jnp.zeros_like(ids)
    for group in range(1, groups):
        owner = owner + jnp.where(ids >= group * entries, 1, 0)
    return owner


def route_kernel(groups, entries, row_ref, list_ref, slot_ref):
    height = row_ref.shape[1]
    ids = row_ref[...]
    lane = lax.broadcasted_iota(jnp.int32, (TILE, height), 1)
    line = lax.broadcasted_iota(jnp.int32, (TILE, height), 0)
    repeat = jnp.zeros((1, height), jnp.int32)
    columns = []
    for start in range(0, height, TILE):
        own_lane = jnp.where(line + start == lane, ids, 0).astype(jnp.float32)
        columns.append(jnp.sum(own_lane, axis=1, keepdims=True).astype(jnp.int32))
        same = (columns[-1] == ids[:, start:]) & (line[:, : height - start] < lane[:, : height - start])
        again = jnp.max(jnp.where(same, 1, 0), axis=0, keepdims=True)
        if start:
            again = jnp.concatenate([jnp.zeros((1, start), jnp.int32), again], axis=1)
        repeat = jnp.maximum(repeat, again)
    fresh = repeat == 0
    owner = owner_of(ids, entries, groups)
    lanes_of = lax.broadcasted_iota(jnp.int32, (groups, height), 0) == owner
    marked = jnp.where(lanes_of & fresh, 1.0, 0.0).astype(jnp.bfloat16)
    rank = jnp.zeros((groups, height), jnp.float32)
    for start in range(0, height, TILE):
        below = jnp.where(line + start < lane, 1.0, 0.0).astype(jnp.bfloat16)
        rank = rank + jnp.dot(
            marked[:, start : start + TILE], below, preferred_element_type=jnp.float32
        )
    place = jnp.sum(jnp.where(lanes_of, rank, 0.0), axis=0, keepdims=True)
    full = jnp.max(jnp.where(fresh, place, 0.0), axis=1, keepdims=True) >= ROOM
    slot = jnp.where(fresh, owner.astype(jnp.float32) * SLOTS + place, 0.0)
    wide = lax.broadcasted_iota(jnp.int32, (TILE, groups * SLOTS), 1)
    wanted = jnp.zeros((1, groups * SLOTS), jnp.int32)
    for start in range(0, height, TILE):
        column = columns[start // TILE]
        mine = jnp.sum(jnp.where(column == ids, slot, 0.0), axis=1, keepdims=True).astype(jnp.int32)
        holder = owner_of(column, entries, groups)
        slot_ref[pl.ds(start, TILE), :] = mine - holder * (SLOTS - ROOM)
        entry = column - holder * entries
        wanted = jnp.maximum(
            wanted, jnp.max(jnp.where(wide == mine, entry, 0), axis=0, keepdims=True)
        )
    place_of = lax.broadcasted_iota(jnp.int32, (1, groups * SLOTS), 1) & (SLOTS - 1)
    list_ref[...] = jnp.where(place_of >= ROOM, jnp.where(full, 1, 0), wanted)


def route(item_ids, groups, entries):
    height = item_ids.shape[1]
    return pl.pallas_call(
        functools.partial(route_kernel, groups, entries),
        out_shape=(
            jax.ShapeDtypeStruct((1, groups * SLOTS), jnp.int32),
            jax.ShapeDtypeStruct((height, 1), jnp.int32),
        ),
        in_specs=[vmem()],
        out_specs=(vmem(), vmem()),
        compiler_params=pltpu.CompilerParams(vmem_limit_bytes=16 * MIB),
        name="route",
    )(item_ids)


def expand_kernel(slot_ref, held_ref, event_ref, normed_ref, head_ref, tail_ref):
    rows = held_ref.shape[0]
    part = TILE
    wide = lax.broadcasted_iota(jnp.int32, (part, rows), 1)

    height = event_ref.shape[0]
    for start in range(0, height, part):
        place = pl.ds(start, part)
        pick = jnp.where(slot_ref[place, :] == wide, 1.0, 0.0).astype(jnp.bfloat16)
        events = jnp.dot(pick, held_ref[...], preferred_element_type=jnp.float32)
        normed = row_norm(events).astype(jnp.bfloat16)
        event_ref[place, :] = events.astype(jnp.bfloat16)
        normed_ref[place, :] = normed
        half_ref = head_ref if start < height // 2 else tail_ref
        half_ref[pl.ds(start % (height // 2), part), :] = normed


def expand(slot, held):
    height, width = slot.shape[0], held.shape[1]
    shape = jax.ShapeDtypeStruct((height, width), jnp.bfloat16)
    part = jax.ShapeDtypeStruct((height // 2, width), jnp.bfloat16)
    return pl.pallas_call(
        expand_kernel,
        out_shape=(shape, shape, part, part),
        in_specs=[vmem(), vmem()],
        out_specs=(vmem(), vmem(), vmem(), vmem()),
        compiler_params=pltpu.CompilerParams(vmem_limit_bytes=16 * MIB),
        name="expand",
    )(slot, held)


def look_up(item_ids, table, w_proj):
    groups = lax.axis_size("batch")
    height = item_ids.shape[1]
    entries, width = table.shape
    wanted, slot = route(item_ids, groups, entries)
    asked = lax.all_to_all(wanted.reshape(groups, SLOTS), "batch", 0, 0, tiled=True)
    crowded = jnp.max(asked[:, ROOM]) > 0
    picked = jnp.take(table, asked[:, :ROOM].reshape(-1), axis=0, mode="clip")
    held = lax.all_to_all(picked, "batch", 0, 0, tiled=True)
    held, w_half = lax.optimization_barrier((held, w_proj * jnp.bfloat16(0.5)))
    found = expand(slot, held)

    def whole():
        every = lax.all_to_all(
            jnp.broadcast_to(item_ids, (groups, height)), "batch", 0, 0, tiled=True
        )
        local = every.reshape(-1) - lax.axis_index("batch") * entries
        dense = jnp.take(table, local, axis=0, mode="clip")
        dense = lax.all_to_all(dense, "batch", 0, 0, tiled=True).reshape(groups, height, width)
        owner = item_ids[0] // entries
        rows = jnp.zeros((height, width), jnp.bfloat16)
        for group in range(groups):
            rows = jnp.where((owner == group)[:, None], dense[group], rows)
        normed = row_norm(rows.astype(jnp.float32)).astype(jnp.bfloat16)
        return rows, normed, normed[: height // 2], normed[height // 2 :]

    return *lax.cond(crowded, whole, lambda: found), w_half


def earlier_tiles(users_ref, tile, most):
    user = users_ref[0, tile]

    def look(back, count):
        at = tile - back
        here = (at >= 0) & (users_ref[0, jnp.maximum(at, 0)] == user)
        return count + jnp.where(here, 1, 0)

    return lax.fori_loop(1, most + 1, look, jnp.int32(0))


def rows_at(tile):
    return pl.ds(pl.multiple_of(tile * TILE, TILE), TILE)


def stack_heads(block, stack_ref, first_tile):
    lane = lax.broadcasted_iota(jnp.int32, (TILE, TILE), 1)
    heads = (lane < TILE // 2, lane >= TILE // 2)
    masks = [jnp.where(head, 1.0, 0.0).astype(jnp.bfloat16) for head in heads]
    for tile in range(block.shape[0] // TILE):
        for at in range(block.shape[1] // TILE):
            both = block[tile * TILE : (tile + 1) * TILE, at * TILE : (at + 1) * TILE]
            for which in range(2):
                place = pl.ds(pl.multiple_of((first_tile + tile) * 2 * TILE, TILE) + which * TILE, TILE)
                stack_ref[at, place, :] = both * masks[which]


def attend(query_ref, key_ref, value_ref, total_ref, rows, places, mask_ref=None, fresh=False):
    for at in range(key_ref.shape[0]):
        columns = slice(at * TILE, (at + 1) * TILE)
        half = lax.dot_general(
            query_ref[rows, columns],
            key_ref[at, places, :],
            (((1,), (1,)), ((), ())),
            preferred_element_type=jnp.float32,
        )
        weights = half_silu(half).astype(jnp.bfloat16)
        if mask_ref is not None:
            weights = weights * mask_ref[...]
        part = jnp.dot(weights, value_ref[at, places, :], preferred_element_type=jnp.float32)
        if fresh:
            total_ref[rows, columns] = part
        else:
            total_ref[rows, columns] += part


def project(normed, proj_ref, at, width):
    half = jnp.dot(
        normed, proj_ref[:, at * width : (at + 1) * width], preferred_element_type=jnp.float32
    )
    return half_silu(half).astype(jnp.bfloat16)


def own_kernel(
    shard_ref,
    users_ref,
    head_ref,
    tail_ref,
    proj_ref,
    gate_ref,
    query_ref,
    total_ref,
    key_ref,
    value_ref,
    mask_ref,
):
    height, width = query_ref.shape
    tiles = height // TILE
    part = height // 2
    base = shard_ref[0, 0] * tiles

    def prepare(half, carry):
        rows = pl.ds(pl.multiple_of(half * part, part), part)
        normed = jnp.where(half == 0, head_ref[...], tail_ref[...])
        gate_ref[rows, :] = project(normed, proj_ref, 0, width)
        query_ref[rows, :] = project(normed, proj_ref, 1, width) * jnp.bfloat16(0.5)
        stack_heads(project(normed, proj_ref, 2, width), key_ref, half * (tiles // 2))
        stack_heads(project(normed, proj_ref, 3, width), value_ref, half * (tiles // 2))
        return carry

    lax.fori_loop(0, 2, prepare, 0)

    line = lax.broadcasted_iota(jnp.int32, (TILE, 2 * part), 0)
    lane = lax.broadcasted_iota(jnp.int32, (TILE, 2 * part), 1)
    key_row = lax.shift_right_logical(lane, 8) * TILE + (lane & (TILE - 1))

    def block(query_half, key_half, fresh):
        def look(tile, carry):
            at = query_half * (tiles // 2) + tile
            first = at - earlier_tiles(users_ref, base + at, tiles - 1)
            least = (first - key_half * (tiles // 2)) * TILE
            most = line + (tile + (query_half - key_half) * (tiles // 2)) * TILE
            seen = (key_row >= least) & (key_row <= most)
            mask_ref[rows_at(tile), :] = jnp.where(seen, 1.0, 0.0).astype(jnp.bfloat16)
            return carry

        lax.fori_loop(0, tiles // 2, look, 0)
        attend(
            query_ref,
            key_ref,
            value_ref,
            total_ref,
            pl.ds(pl.multiple_of(query_half * part, part), part),
            pl.ds(pl.multiple_of(key_half * 2 * part, part), 2 * part),
            mask_ref,
            fresh,
        )

    def same(half, carry):
        block(half, half, True)
        return carry

    lax.fori_loop(0, 2, same, 0)
    middle = base + tiles // 2

    @pl.when(users_ref[0, middle] == users_ref[0, middle - 1])
    def _():
        block(1, 0, False)


def own(shard, users, head, tail, w_proj):
    height, width = 2 * head.shape[0], head.shape[1]
    tiles, pairs = height // TILE, width // TILE
    return pl.pallas_call(
        own_kernel,
        out_shape=(
            jax.ShapeDtypeStruct((height, width), jnp.bfloat16),
            jax.ShapeDtypeStruct((height, width), jnp.bfloat16),
            jax.ShapeDtypeStruct((height, width), jnp.float32),
        ),
        in_specs=[smem(), smem(), vmem(), vmem(), vmem()],
        out_specs=(vmem(), vmem(), vmem()),
        scratch_shapes=[
            pltpu.VMEM((pairs, tiles * 2 * TILE, TILE), jnp.bfloat16),
            pltpu.VMEM((pairs, tiles * 2 * TILE, TILE), jnp.bfloat16),
            pltpu.VMEM((height // 2, height), jnp.bfloat16),
        ],
        compiler_params=pltpu.CompilerParams(vmem_limit_bytes=24 * MIB),
        cost_estimate=pl.CostEstimate(flops=10**6, bytes_accessed=10**5, transcendentals=0),
        name="own",
    )(shard, users, head, tail, w_proj)


def add_half(
    normed, half, begin, asking, proj_ref, query_ref, total_ref, key_ref, value_ref
):
    part, width = normed.shape
    line = lax.broadcasted_iota(jnp.int32, (part, width), 0) + half * part
    values = project(normed, proj_ref, 1, width)
    values = jnp.where(line >= begin, values.astype(jnp.float32), 0.0)
    stack_heads(project(normed, proj_ref, 0, width), key_ref, 0)
    stack_heads(values.astype(jnp.bfloat16), value_ref, 0)

    def query(at, carry):
        attend(
            query_ref,
            key_ref,
            value_ref,
            total_ref,
            pl.ds(pl.multiple_of(at * part, part), part),
            pl.ds(0, 2 * part),
        )
        return carry

    lax.fori_loop(0, jnp.where(asking * TILE > part, 2, 1), query, 0)


def add_earlier(
    block_of, distance, needed, asking, proj_ref, query_ref, total_ref, key_ref, value_ref
):
    height = query_ref.shape[0]
    part = height // 2
    used = used_of(needed, distance, height // TILE)

    @pl.when(used > 0)
    def _():
        total_ref[...] = jnp.zeros_like(total_ref)

    def each(half, carry):
        add_half(
            block_of(half),
            half,
            height - used * TILE,
            asking,
            proj_ref,
            query_ref,
            total_ref,
            key_ref,
            value_ref,
        )
        return carry

    lax.fori_loop(jnp.where(used * TILE > part, 0, 1), jnp.where(used > 0, 2, 0), each, 0)


def used_of(needed, distance, tiles):
    return jnp.clip(needed - tiles * (distance - 1), 0, tiles)


def reach(shard_ref, users_ref, tiles):
    base = shard_ref[0, 0] * tiles
    needed = earlier_tiles(users_ref, base, (REACH - 1) * tiles)
    asking = jnp.int32(0)
    for tile in range(tiles):
        asking = asking + jnp.where(users_ref[0, base + tile] == users_ref[0, base], 1, 0)
    return base, needed, asking


def early_kernel(
    half,
    shard_ref,
    users_ref,
    proj_ref,
    query_ref,
    block_ref,
    total_ref,
    key_ref,
    value_ref,
):
    height = query_ref.shape[0]
    _, needed, asking = reach(shard_ref, users_ref, height // TILE)
    used = used_of(needed, 2, height // TILE)

    @pl.when(used * TILE > height // 2 * (1 - half))
    def _():
        total_ref[...] = jnp.zeros_like(total_ref)
        add_half(
            block_ref[...],
            half,
            height - used * TILE,
            asking,
            proj_ref,
            query_ref,
            total_ref,
            key_ref,
            value_ref,
        )


def middle_kernel(
    shard_ref,
    users_ref,
    proj_ref,
    query_ref,
    block_ref,
    total_ref,
    key_ref,
    value_ref,
):
    part = query_ref.shape[0] // 2

    def block_of(half):
        return block_ref[pl.ds(pl.multiple_of(half * part, part), part), :]

    _, needed, asking = reach(shard_ref, users_ref, query_ref.shape[0] // TILE)
    add_earlier(
        block_of,
        3 - 2 * lax.rem(shard_ref[0, 0], 2),
        needed,
        asking,
        proj_ref,
        query_ref,
        total_ref,
        key_ref,
        value_ref,
    )


def late_kernel(
    shard_ref,
    users_ref,
    pad_ref,
    head_ref,
    tail_ref,
    proj_ref,
    query_ref,
    gate_ref,
    own_ref,
    early_tail_ref,
    early_head_ref,
    middle_ref,
    event_ref,
    out_proj_ref,
    out_ref,
    total_ref,
    key_ref,
    value_ref,
):
    height, width = query_ref.shape
    tiles = height // TILE
    count = users_ref.shape[1]
    base, needed, asking = reach(shard_ref, users_ref, tiles)
    core = lax.rem(shard_ref[0, 0], 2)

    def block_of(half):
        return jnp.where(half == 0, head_ref[...], tail_ref[...])

    add_earlier(
        block_of,
        1 + 2 * core,
        needed,
        asking,
        proj_ref,
        query_ref,
        total_ref,
        key_ref,
        value_ref,
    )
    parts = (
        (early_tail_ref, used_of(needed, 2, tiles)),
        (early_head_ref, used_of(needed, 2, tiles) - tiles // 2),
        (middle_ref, used_of(needed, 3 - 2 * core, tiles)),
        (total_ref, used_of(needed, 1 + 2 * core, tiles)),
    )
    part = height // 2

    line = lax.broadcasted_iota(jnp.int32, (TILE, width), 0)

    def finish(half, carry):
        rows = pl.ds(pl.multiple_of(half * part, part), part)
        inside = lax.broadcasted_iota(jnp.int32, (part, width), 0) + half * part
        attended = own_ref[rows, :]
        for ref, used in parts:
            limit = jnp.where(used > 0, asking * TILE, 0)
            attended = attended + jnp.where(inside < limit, ref[rows, :], 0.0)
        gated = row_norm(attended) * gate_ref[rows, :].astype(jnp.float32)
        mixed = jnp.dot(
            gated.astype(jnp.bfloat16), out_proj_ref[...], preferred_element_type=jnp.float32
        ) + event_ref[rows, :].astype(jnp.float32)
        for tile in range(tiles // 2):
            at = base + half * (tiles // 2) + tile
            here = users_ref[0, at]
            last = (at == count - 1) | (users_ref[0, jnp.minimum(at + 1, count - 1)] != here)
            limit = TILE - jnp.where(last, pad_ref[0, here], 0)
            kept = jnp.where(line < limit, mixed[tile * TILE : (tile + 1) * TILE], 0.0)
            out_ref[rows_at(half * (tiles // 2) + tile), :] = kept.astype(jnp.bfloat16)
        return carry

    lax.fori_loop(0, 2, finish, 0, unroll=True)


def scratch_of(height, width):
    tiles, pairs = height // TILE // 2, width // TILE
    return [
        pltpu.VMEM((pairs, tiles * 2 * TILE, TILE), jnp.bfloat16),
        pltpu.VMEM((pairs, tiles * 2 * TILE, TILE), jnp.bfloat16),
    ]


def earlier_part(kernel, name, flops, shard, users, w_keys_values, queries, *blocks):
    height, width = queries.shape
    return pl.pallas_call(
        kernel,
        out_shape=jax.ShapeDtypeStruct((height, width), jnp.float32),
        in_specs=[smem()] * 2 + [vmem()] * (2 + len(blocks)),
        out_specs=vmem(),
        scratch_shapes=scratch_of(height, width),
        compiler_params=pltpu.CompilerParams(vmem_limit_bytes=24 * MIB),
        cost_estimate=pl.CostEstimate(flops=flops, bytes_accessed=10**5, transcendentals=0),
        name=name,
    )(shard, users, w_keys_values, queries, *blocks)


def late(shard, users, pad, *arrays):
    height, width = arrays[3].shape
    return pl.pallas_call(
        late_kernel,
        out_shape=jax.ShapeDtypeStruct((height, width), jnp.bfloat16),
        in_specs=[smem()] * 3 + [vmem()] * len(arrays),
        out_specs=vmem(),
        scratch_shapes=[pltpu.VMEM((height, width), jnp.float32)] + scratch_of(height, width),
        compiler_params=pltpu.CompilerParams(vmem_limit_bytes=24 * MIB),
        cost_estimate=pl.CostEstimate(
            flops=8 * 10**9, bytes_accessed=10 * 10**6, transcendentals=4 * 10**6
        ),
        name="late",
    )(shard, users, pad, *arrays)


def on_device(item_ids, table, tile_user, tail_pad, w_proj, w_out):
    shards = lax.axis_size("seq")
    shard = lax.axis_index("seq").astype(jnp.int32).reshape(1, 1)
    events, normed, head, tail, w_half = look_up(item_ids, table, w_proj)
    apart = [(i, i + 1 if i % 2 == 0 else i + 3) for i in range(shards)]
    ahead = [(i, i + 2) for i in range(shards - 2)]
    cores = [(i, i ^ 1) for i in range(shards)]
    mid_tail = lax.ppermute(tail, "seq", ahead)
    mid_head = lax.ppermute(head, "seq", ahead)
    apart = [(i, j) for i, j in apart if j < shards]
    odd = lax.ppermute(normed, "seq", apart)
    gate, queries, total = own(shard, tile_user, head, tail, w_half)
    w_keys_values = w_half[:, w_half.shape[1] // 2 :]

    def part_of(kernel, name, flops, *blocks):
        return earlier_part(kernel, name, flops, shard, tile_user, w_keys_values, queries, *blocks)

    mid_tail, queries = lax.optimization_barrier((mid_tail, queries))
    swap_tail = lax.ppermute(mid_tail, "seq", cores)
    early_tail = part_of(functools.partial(early_kernel, 1), "early_tail", 10**6, mid_tail)
    mid_head, early_tail = lax.optimization_barrier((mid_head, early_tail))
    swap_head = lax.ppermute(mid_head, "seq", cores)
    early_head = part_of(functools.partial(early_kernel, 0), "early_head", 5 * 10**9, mid_head)
    odd, early_head = lax.optimization_barrier((odd, early_head))
    middle = part_of(middle_kernel, "middle", 8 * 10**9, odd)
    swap_head, swap_tail, middle = lax.optimization_barrier((swap_head, swap_tail, middle))
    mixed = late(
        shard,
        tile_user,
        tail_pad,
        swap_head,
        swap_tail,
        w_keys_values,
        queries,
        gate,
        total,
        early_tail,
        early_head,
        middle,
        events,
        w_out,
    )
    return mixed[None]


def solution(mesh):
    in_specs = (P("batch", "seq"), P("batch", None), P("batch", None), P("batch", None), P(), P())
    out_specs = P("batch", "seq", None)
    return jax.shard_map(
        on_device, mesh=mesh, in_specs=in_specs, out_specs=out_specs, check_vma=False
    )
```

```python
import functools

import jax
import jax.numpy as jnp
from jax import lax
from jax.experimental import pallas as pl
from jax.experimental.pallas import tpu as pltpu
from jax.sharding import PartitionSpec as P

HEADS = 8
TILE = 128
REACH = 4
ROOM = 96
SLOTS = 128
MIB = 1 << 20


def vmem():
    return pl.BlockSpec(memory_space=pltpu.VMEM)


def smem():
    return pl.BlockSpec(memory_space=pltpu.SMEM)


def row_norm(values):
    center = values - jnp.mean(values, axis=-1, keepdims=True)
    spread = jnp.mean(center * center, axis=-1, keepdims=True)
    return center * lax.rsqrt(spread + 1e-05)


def half_silu(half):
    return half + half * jnp.tanh(half)


def owner_of(ids, entries, groups):
    owner = jnp.zeros_like(ids)
    for group in range(1, groups):
        owner = owner + jnp.where(ids >= group * entries, 1, 0)
    return owner


def route_kernel(groups, entries, row_ref, list_ref, slot_ref):
    height = row_ref.shape[1]
    ids = row_ref[...]
    lane = lax.broadcasted_iota(jnp.int32, (TILE, height), 1)
    line = lax.broadcasted_iota(jnp.int32, (TILE, height), 0)
    repeat = jnp.zeros((1, height), jnp.int32)
    columns = []
    for start in range(0, height, TILE):
        own_lane = jnp.where(line + start == lane, ids, 0).astype(jnp.float32)
        columns.append(jnp.sum(own_lane, axis=1, keepdims=True).astype(jnp.int32))
        same = (columns[-1] == ids[:, start:]) & (line[:, : height - start] < lane[:, : height - start])
        again = jnp.max(jnp.where(same, 1, 0), axis=0, keepdims=True)
        if start:
            again = jnp.concatenate([jnp.zeros((1, start), jnp.int32), again], axis=1)
        repeat = jnp.maximum(repeat, again)
    fresh = repeat == 0
    owner = owner_of(ids, entries, groups)
    lanes_of = lax.broadcasted_iota(jnp.int32, (groups, height), 0) == owner
    marked = jnp.where(lanes_of & fresh, 1.0, 0.0).astype(jnp.bfloat16)
    rank = jnp.zeros((groups, height), jnp.float32)
    for start in range(0, height, TILE):
        below = jnp.where(line + start < lane, 1.0, 0.0).astype(jnp.bfloat16)
        rank = rank + jnp.dot(
            marked[:, start : start + TILE], below, preferred_element_type=jnp.float32
        )
    place = jnp.sum(jnp.where(lanes_of, rank, 0.0), axis=0, keepdims=True)
    full = jnp.max(jnp.where(fresh, place, 0.0), axis=1, keepdims=True) >= ROOM
    slot = jnp.where(fresh, owner.astype(jnp.float32) * SLOTS + place, 0.0)
    wide = lax.broadcasted_iota(jnp.int32, (TILE, groups * SLOTS), 1)
    wanted = jnp.zeros((1, groups * SLOTS), jnp.int32)
    for start in range(0, height, TILE):
        column = columns[start // TILE]
        mine = jnp.sum(jnp.where(column == ids, slot, 0.0), axis=1, keepdims=True).astype(jnp.int32)
        holder = owner_of(column, entries, groups)
        slot_ref[pl.ds(start, TILE), :] = mine - holder * (SLOTS - ROOM)
        entry = column - holder * entries
        wanted = jnp.maximum(
            wanted, jnp.max(jnp.where(wide == mine, entry, 0), axis=0, keepdims=True)
        )
    place_of = lax.broadcasted_iota(jnp.int32, (1, groups * SLOTS), 1) & (SLOTS - 1)
    list_ref[...] = jnp.where(place_of >= ROOM, jnp.where(full, 1, 0), wanted)


def route(item_ids, groups, entries):
    height = item_ids.shape[1]
    return pl.pallas_call(
        functools.partial(route_kernel, groups, entries),
        out_shape=(
            jax.ShapeDtypeStruct((1, groups * SLOTS), jnp.int32),
            jax.ShapeDtypeStruct((height, 1), jnp.int32),
        ),
        in_specs=[vmem()],
        out_specs=(vmem(), vmem()),
        compiler_params=pltpu.CompilerParams(vmem_limit_bytes=16 * MIB),
        name="route",
    )(item_ids)


def expand_kernel(slot_ref, held_ref, event_ref, normed_ref, mine_ref, head_ref, tail_ref):
    rows = held_ref.shape[0]
    part = TILE
    wide = lax.broadcasted_iota(jnp.int32, (part, rows), 1)

    height = event_ref.shape[0]
    for start in range(0, height, part):
        place = pl.ds(start, part)
        pick = jnp.where(slot_ref[place, :] == wide, 1.0, 0.0).astype(jnp.bfloat16)
        events = jnp.dot(pick, held_ref[...], preferred_element_type=jnp.float32)
        normed = row_norm(events).astype(jnp.bfloat16)
        event_ref[place, :] = events.astype(jnp.bfloat16)
        normed_ref[place, :] = normed
        mine_ref[place, :] = normed
        half_ref = head_ref if start < height // 2 else tail_ref
        half_ref[pl.ds(start % (height // 2), part), :] = normed


def expand(slot, held):
    height, width = slot.shape[0], held.shape[1]
    shape = jax.ShapeDtypeStruct((height, width), jnp.bfloat16)
    part = jax.ShapeDtypeStruct((height // 2, width), jnp.bfloat16)
    return pl.pallas_call(
        expand_kernel,
        out_shape=(shape, shape, shape, part, part),
        in_specs=[vmem(), vmem()],
        out_specs=(vmem(), vmem(), vmem(), vmem(), vmem()),
        compiler_params=pltpu.CompilerParams(vmem_limit_bytes=16 * MIB),
        name="expand",
    )(slot, held)


def look_up(item_ids, table, w_proj):
    groups = lax.axis_size("batch")
    height = item_ids.shape[1]
    entries, width = table.shape
    wanted, slot = route(item_ids, groups, entries)
    asked = lax.all_to_all(wanted.reshape(groups, SLOTS), "batch", 0, 0, tiled=True)
    crowded = jnp.max(asked[:, ROOM]) > 0
    picked = jnp.take(table, asked[:, :ROOM].reshape(-1), axis=0, mode="clip")
    held = lax.all_to_all(picked, "batch", 0, 0, tiled=True)
    held, w_half = lax.optimization_barrier((held, w_proj * jnp.bfloat16(0.5)))
    found = expand(slot, held)

    def whole():
        every = lax.all_to_all(
            jnp.broadcast_to(item_ids, (groups, height)), "batch", 0, 0, tiled=True
        )
        local = every.reshape(-1) - lax.axis_index("batch") * entries
        dense = jnp.take(table, local, axis=0, mode="clip")
        dense = lax.all_to_all(dense, "batch", 0, 0, tiled=True).reshape(groups, height, width)
        owner = item_ids[0] // entries
        rows = jnp.zeros((height, width), jnp.bfloat16)
        for group in range(groups):
            rows = jnp.where((owner == group)[:, None], dense[group], rows)
        normed = row_norm(rows.astype(jnp.float32)).astype(jnp.bfloat16)
        return rows, normed, normed, normed[: height // 2], normed[height // 2 :]

    return *lax.cond(crowded, whole, lambda: found), w_half


def earlier_tiles(users_ref, tile, most):
    user = users_ref[0, tile]

    def look(back, count):
        at = tile - back
        here = (at >= 0) & (users_ref[0, jnp.maximum(at, 0)] == user)
        return count + jnp.where(here, 1, 0)

    return lax.fori_loop(1, most + 1, look, jnp.int32(0))


def rows_at(tile):
    return pl.ds(pl.multiple_of(tile * TILE, TILE), TILE)


def stack_heads(block, stack_ref, first_tile):
    lane = lax.broadcasted_iota(jnp.int32, (TILE, TILE), 1)
    heads = (lane < TILE // 2, lane >= TILE // 2)
    masks = [jnp.where(head, 1.0, 0.0).astype(jnp.bfloat16) for head in heads]
    for tile in range(block.shape[0] // TILE):
        for at in range(block.shape[1] // TILE):
            both = block[tile * TILE : (tile + 1) * TILE, at * TILE : (at + 1) * TILE]
            for which in range(2):
                place = pl.ds(pl.multiple_of((first_tile + tile) * 2 * TILE, TILE) + which * TILE, TILE)
                stack_ref[at, place, :] = both * masks[which]


def attend(query_ref, key_ref, value_ref, total_ref, rows, places, mask_ref=None, fresh=False):
    for at in range(key_ref.shape[0]):
        columns = slice(at * TILE, (at + 1) * TILE)
        half = lax.dot_general(
            query_ref[rows, columns],
            key_ref[at, places, :],
            (((1,), (1,)), ((), ())),
            preferred_element_type=jnp.float32,
        )
        weights = half_silu(half).astype(jnp.bfloat16)
        if mask_ref is not None:
            weights = weights * mask_ref[...]
        part = jnp.dot(weights, value_ref[at, places, :], preferred_element_type=jnp.float32)
        if fresh:
            total_ref[rows, columns] = part
        else:
            total_ref[rows, columns] += part


def project(normed, proj_ref, at, width):
    half = jnp.dot(
        normed, proj_ref[:, at * width : (at + 1) * width], preferred_element_type=jnp.float32
    )
    return half_silu(half).astype(jnp.bfloat16)


def own_kernel(
    shard_ref,
    users_ref,
    normed_ref,
    proj_ref,
    gate_ref,
    query_ref,
    total_ref,
    key_ref,
    value_ref,
    mask_ref,
):
    height, width = query_ref.shape
    tiles = height // TILE
    part = height // 2
    base = shard_ref[0, 0] * tiles

    def prepare(half, carry):
        rows = pl.ds(pl.multiple_of(half * part, part), part)
        normed = normed_ref[rows, :]
        gate_ref[rows, :] = project(normed, proj_ref, 0, width)
        query_ref[rows, :] = project(normed, proj_ref, 1, width) * jnp.bfloat16(0.5)
        stack_heads(project(normed, proj_ref, 2, width), key_ref, half * (tiles // 2))
        stack_heads(project(normed, proj_ref, 3, width), value_ref, half * (tiles // 2))
        return carry

    lax.fori_loop(0, 2, prepare, 0)

    line = lax.broadcasted_iota(jnp.int32, (TILE, 2 * part), 0)
    lane = lax.broadcasted_iota(jnp.int32, (TILE, 2 * part), 1)
    key_row = lax.shift_right_logical(lane, 8) * TILE + (lane & (TILE - 1))

    def block(query_half, key_half, fresh):
        def look(tile, carry):
            at = query_half * (tiles // 2) + tile
            first = at - earlier_tiles(users_ref, base + at, tiles - 1)
            least = (first - key_half * (tiles // 2)) * TILE
            most = line + (tile + (query_half - key_half) * (tiles // 2)) * TILE
            seen = (key_row >= least) & (key_row <= most)
            mask_ref[rows_at(tile), :] = jnp.where(seen, 1.0, 0.0).astype(jnp.bfloat16)
            return carry

        lax.fori_loop(0, tiles // 2, look, 0)
        attend(
            query_ref,
            key_ref,
            value_ref,
            total_ref,
            pl.ds(pl.multiple_of(query_half * part, part), part),
            pl.ds(pl.multiple_of(key_half * 2 * part, part), 2 * part),
            mask_ref,
            fresh,
        )

    def same(half, carry):
        block(half, half, True)
        return carry

    lax.fori_loop(0, 2, same, 0)
    middle = base + tiles // 2

    @pl.when(users_ref[0, middle] == users_ref[0, middle - 1])
    def _():
        block(1, 0, False)


def own(shard, users, normed, w_proj):
    height, width = normed.shape
    tiles, pairs = height // TILE, width // TILE
    return pl.pallas_call(
        own_kernel,
        out_shape=(
            jax.ShapeDtypeStruct((height, width), jnp.bfloat16),
            jax.ShapeDtypeStruct((height, width), jnp.bfloat16),
            jax.ShapeDtypeStruct((height, width), jnp.float32),
        ),
        in_specs=[smem(), smem(), vmem(), vmem()],
        out_specs=(vmem(), vmem(), vmem()),
        scratch_shapes=[
            pltpu.VMEM((pairs, tiles * 2 * TILE, TILE), jnp.bfloat16),
            pltpu.VMEM((pairs, tiles * 2 * TILE, TILE), jnp.bfloat16),
            pltpu.VMEM((height // 2, height), jnp.bfloat16),
        ],
        compiler_params=pltpu.CompilerParams(vmem_limit_bytes=24 * MIB),
        cost_estimate=pl.CostEstimate(flops=10**6, bytes_accessed=10**5, transcendentals=0),
        name="own",
    )(shard, users, normed, w_proj)


def add_half(
    normed, half, begin, asking, proj_ref, query_ref, total_ref, key_ref, value_ref
):
    part, width = normed.shape
    line = lax.broadcasted_iota(jnp.int32, (part, width), 0) + half * part
    values = project(normed, proj_ref, 1, width)
    values = jnp.where(line >= begin, values.astype(jnp.float32), 0.0)
    stack_heads(project(normed, proj_ref, 0, width), key_ref, 0)
    stack_heads(values.astype(jnp.bfloat16), value_ref, 0)

    def query(at, carry):
        attend(
            query_ref,
            key_ref,
            value_ref,
            total_ref,
            pl.ds(pl.multiple_of(at * part, part), part),
            pl.ds(0, 2 * part),
        )
        return carry

    lax.fori_loop(0, jnp.where(asking * TILE > part, 2, 1), query, 0)


def add_earlier(
    block_of, distance, needed, asking, proj_ref, query_ref, total_ref, key_ref, value_ref
):
    height = query_ref.shape[0]
    part = height // 2
    used = used_of(needed, distance, height // TILE)

    @pl.when(used > 0)
    def _():
        total_ref[...] = jnp.zeros_like(total_ref)

    def each(half, carry):
        add_half(
            block_of(half),
            half,
            height - used * TILE,
            asking,
            proj_ref,
            query_ref,
            total_ref,
            key_ref,
            value_ref,
        )
        return carry

    lax.fori_loop(jnp.where(used * TILE > part, 0, 1), jnp.where(used > 0, 2, 0), each, 0)


def used_of(needed, distance, tiles):
    return jnp.clip(needed - tiles * (distance - 1), 0, tiles)


def reach(shard_ref, users_ref, tiles):
    base = shard_ref[0, 0] * tiles
    needed = earlier_tiles(users_ref, base, (REACH - 1) * tiles)
    asking = jnp.int32(0)
    for tile in range(tiles):
        asking = asking + jnp.where(users_ref[0, base + tile] == users_ref[0, base], 1, 0)
    return base, needed, asking


def early_kernel(
    half,
    shard_ref,
    users_ref,
    proj_ref,
    query_ref,
    block_ref,
    total_ref,
    key_ref,
    value_ref,
):
    height = query_ref.shape[0]
    _, needed, asking = reach(shard_ref, users_ref, height // TILE)
    used = used_of(needed, 2, height // TILE)

    @pl.when(used * TILE > height // 2 * (1 - half))
    def _():
        total_ref[...] = jnp.zeros_like(total_ref)
        add_half(
            block_ref[...],
            half,
            height - used * TILE,
            asking,
            proj_ref,
            query_ref,
            total_ref,
            key_ref,
            value_ref,
        )


def middle_kernel(
    shard_ref,
    users_ref,
    proj_ref,
    query_ref,
    block_ref,
    total_ref,
    key_ref,
    value_ref,
):
    part = query_ref.shape[0] // 2

    def block_of(half):
        return block_ref[pl.ds(pl.multiple_of(half * part, part), part), :]

    _, needed, asking = reach(shard_ref, users_ref, query_ref.shape[0] // TILE)
    add_earlier(
        block_of,
        3 - 2 * lax.rem(shard_ref[0, 0], 2),
        needed,
        asking,
        proj_ref,
        query_ref,
        total_ref,
        key_ref,
        value_ref,
    )


def late_kernel(
    shard_ref,
    users_ref,
    pad_ref,
    head_ref,
    tail_ref,
    proj_ref,
    query_ref,
    gate_ref,
    own_ref,
    early_tail_ref,
    early_head_ref,
    middle_ref,
    event_ref,
    out_proj_ref,
    out_ref,
    total_ref,
    key_ref,
    value_ref,
):
    height, width = query_ref.shape
    tiles = height // TILE
    count = users_ref.shape[1]
    base, needed, asking = reach(shard_ref, users_ref, tiles)
    core = lax.rem(shard_ref[0, 0], 2)

    def block_of(half):
        return jnp.where(half == 0, head_ref[...], tail_ref[...])

    add_earlier(
        block_of,
        1 + 2 * core,
        needed,
        asking,
        proj_ref,
        query_ref,
        total_ref,
        key_ref,
        value_ref,
    )
    parts = (
        (early_tail_ref, used_of(needed, 2, tiles)),
        (early_head_ref, used_of(needed, 2, tiles) - tiles // 2),
        (middle_ref, used_of(needed, 3 - 2 * core, tiles)),
        (total_ref, used_of(needed, 1 + 2 * core, tiles)),
    )
    part = height // 2

    line = lax.broadcasted_iota(jnp.int32, (TILE, width), 0)

    def finish(half, carry):
        rows = pl.ds(pl.multiple_of(half * part, part), part)
        inside = lax.broadcasted_iota(jnp.int32, (part, width), 0) + half * part
        attended = own_ref[rows, :]
        for ref, used in parts:
            limit = jnp.where(used > 0, asking * TILE, 0)
            attended = attended + jnp.where(inside < limit, ref[rows, :], 0.0)
        gated = row_norm(attended) * gate_ref[rows, :].astype(jnp.float32)
        mixed = jnp.dot(
            gated.astype(jnp.bfloat16), out_proj_ref[...], preferred_element_type=jnp.float32
        ) + event_ref[rows, :].astype(jnp.float32)
        for tile in range(tiles // 2):
            at = base + half * (tiles // 2) + tile
            here = users_ref[0, at]
            last = (at == count - 1) | (users_ref[0, jnp.minimum(at + 1, count - 1)] != here)
            limit = TILE - jnp.where(last, pad_ref[0, here], 0)
            kept = jnp.where(line < limit, mixed[tile * TILE : (tile + 1) * TILE], 0.0)
            out_ref[rows_at(half * (tiles // 2) + tile), :] = kept.astype(jnp.bfloat16)
        return carry

    lax.fori_loop(0, 2, finish, 0, unroll=True)


def scratch_of(height, width):
    tiles, pairs = height // TILE // 2, width // TILE
    return [
        pltpu.VMEM((pairs, tiles * 2 * TILE, TILE), jnp.bfloat16),
        pltpu.VMEM((pairs, tiles * 2 * TILE, TILE), jnp.bfloat16),
    ]


def earlier_part(kernel, name, flops, shard, users, w_keys_values, queries, *blocks):
    height, width = queries.shape
    return pl.pallas_call(
        kernel,
        out_shape=jax.ShapeDtypeStruct((height, width), jnp.float32),
        in_specs=[smem()] * 2 + [vmem()] * (2 + len(blocks)),
        out_specs=vmem(),
        scratch_shapes=scratch_of(height, width),
        compiler_params=pltpu.CompilerParams(vmem_limit_bytes=24 * MIB),
        cost_estimate=pl.CostEstimate(flops=flops, bytes_accessed=10**5, transcendentals=0),
        name=name,
    )(shard, users, w_keys_values, queries, *blocks)


def late(shard, users, pad, *arrays):
    height, width = arrays[3].shape
    return pl.pallas_call(
        late_kernel,
        out_shape=jax.ShapeDtypeStruct((height, width), jnp.bfloat16),
        in_specs=[smem()] * 3 + [vmem()] * len(arrays),
        out_specs=vmem(),
        scratch_shapes=[pltpu.VMEM((height, width), jnp.float32)] + scratch_of(height, width),
        compiler_params=pltpu.CompilerParams(vmem_limit_bytes=24 * MIB),
        cost_estimate=pl.CostEstimate(
            flops=8 * 10**9, bytes_accessed=10 * 10**6, transcendentals=4 * 10**6
        ),
        name="late",
    )(shard, users, pad, *arrays)


def on_device(item_ids, table, tile_user, tail_pad, w_proj, w_out):
    shards = lax.axis_size("seq")
    shard = lax.axis_index("seq").astype(jnp.int32).reshape(1, 1)
    events, normed, mine, head, tail, w_half = look_up(item_ids, table, w_proj)
    apart = [(i, i + 1 if i % 2 == 0 else i + 3) for i in range(shards)]
    ahead = [(i, i + 2) for i in range(shards - 2)]
    cores = [(i, i ^ 1) for i in range(shards)]
    mid_tail = lax.ppermute(tail, "seq", ahead)
    mid_head = lax.ppermute(head, "seq", ahead)
    apart = [(i, j) for i, j in apart if j < shards]
    odd = lax.ppermute(normed, "seq", apart)
    gate, queries, total = own(shard, tile_user, mine, w_half)
    w_keys_values = w_half[:, w_half.shape[1] // 2 :]

    def part_of(kernel, name, flops, *blocks):
        return earlier_part(kernel, name, flops, shard, tile_user, w_keys_values, queries, *blocks)

    mid_tail, queries = lax.optimization_barrier((mid_tail, queries))
    swap_tail = lax.ppermute(mid_tail, "seq", cores)
    early_tail = part_of(functools.partial(early_kernel, 1), "early_tail", 10**6, mid_tail)
    mid_head, early_tail = lax.optimization_barrier((mid_head, early_tail))
    swap_head = lax.ppermute(mid_head, "seq", cores)
    early_head = part_of(functools.partial(early_kernel, 0), "early_head", 5 * 10**9, mid_head)
    odd, early_head = lax.optimization_barrier((odd, early_head))
    middle = part_of(middle_kernel, "middle", 8 * 10**9, odd)
    swap_head, swap_tail, middle = lax.optimization_barrier((swap_head, swap_tail, middle))
    mixed = late(
        shard,
        tile_user,
        tail_pad,
        swap_head,
        swap_tail,
        w_keys_values,
        queries,
        gate,
        total,
        early_tail,
        early_head,
        middle,
        events,
        w_out,
    )
    return mixed[None]


def solution(mesh):
    in_specs = (P("batch", "seq"), P("batch", None), P("batch", None), P("batch", None), P(), P())
    out_specs = P("batch", "seq", None)
    return jax.shard_map(
        on_device, mesh=mesh, in_specs=in_specs, out_specs=out_specs, check_vma=False
    )
```
